512 devices in a mesh: lat: 32 (over y, z_lo), lon: 16 (over z_hi, x, core).
Axes of the slice: x: 4, y: 4, z: 16 (z_hi: 2, z_lo: 8; z = z_hi * 8 + z_lo), core: 2. Of those that a mesh axis runs over, the one named last changes fastest.
Arguments:
- field: bfloat16 [512, 512, 256], P('lat', 'lon'), may hold values from -6 to 6
- cotangent: bfloat16 [512, 512, 256], P('lat', 'lon'), may hold values from -6 to 6
- kernel: bfloat16 [9, 256, 256], replicated, may hold values from -0.125 to 0.125
- timestep: int32 [1], replicated, may hold values from 0 to 999
- time_weight: float32 [256, 256], replicated, may hold values from -0.375 to 0.375
- norm_gain: float32 [256], replicated, may hold values from 0.1 to 1.9
- w_query: bfloat16 [256, 256], replicated, may hold values from -1.5 to 1.5
- w_key: bfloat16 [256, 256], replicated, may hold values from -0.375 to 0.375
- w_value: bfloat16 [256, 256], replicated, may hold values from -0.375 to 0.375
- w_out: bfloat16 [256, 256], replicated, may hold values from -0.375 to 0.375
Outputs:
- block_out: bfloat16 [512, 512, 256], P('lat', 'lon')
- grad_field: bfloat16 [512, 512, 256], P('lat', 'lon')
- grad_kernel: float32 [9, 256, 256], P(None, 'lat', 'lon')
- attended: bfloat16 [64, 64, 256], P('lat', 'lon')
The draws below stay inside these ranges and needn't reach their ends.
All inputs are finite; a program needn't handle non-finite values.
Results may differ from the reference program's by a relative error of at most 0.008.
Values may be sent and summed in bfloat16 or wider, within the bound.
A program may use at most 128 MiB of HBM per device.

```python
import math
import jax
import jax.numpy as jnp
from jax import lax

C = 256
HEAD_DIM = 64
TE = 256
POOL = 8
NH = 512
NW = 512
TH = 64
TW = 64


def draw_field(key, part):
    key = jax.random.fold_in(key, 11)
    rough_key, level_key = jax.random.split(key)
    rough_part = jax.random.normal(rough_key, (NH, NW, C), jnp.float32)
    block_levels = 1.5 * jax.random.normal(level_key, (TH, TW, C), jnp.float32)
    widened = jnp.repeat(jnp.repeat(block_levels, POOL, axis=0), POOL, axis=1)
    return jnp.clip(rough_part + widened, -6.0, 6.0).astype(jnp.bfloat16)


def levels(key, shape, cuts, least, largest):
    loudness, own = 1.0, jax.random.fold_in(key, 6)
    for position, shards_of in cuts:
        draws = jnp.exp(jax.random.uniform(jax.random.fold_in(own, position), (shards_of,), jnp.float32, least / len(cuts), largest / len(cuts)))
        loudness = loudness * jnp.repeat(draws, shape[position] // shards_of).reshape([-1 if axis == position else 1 for axis in range(len(shape))])
    return loudness


def centred(own_key, shape, scale, reach, cuts=(), kind=jnp.bfloat16):
    array = jax.random.normal(own_key, shape, jnp.float32) * scale
    if len(cuts) > 0:
        array = levels(own_key, shape, cuts, -0.22, 0.18) * array
    return jnp.clip(array, min=-reach, max=reach).astype(kind)


def setup_inputs(seed: int = 0) -> dict:
    splits = jax.random.split(jax.random.key(seed), 11)
    return {
        "field": draw_field(jax.random.fold_in(splits[10], 71), 0),
        "cotangent": centred(splits[1], (NH, NW, C), 1.0, 6.0, ((0, 32), (1, 16))),
        "kernel": centred(splits[2], (9, C, C), (9 * C) ** -0.5, 0.125),
        "timestep": jax.random.randint(splits[3], (1,), 0, 1000).astype(jnp.int32),
        "time_weight": centred(splits[4], (TE, C), TE ** -0.5, 0.375, (), jnp.float32),
        "norm_gain": jnp.clip(1.0 + 0.18 * jax.random.normal(splits[5], (C,), jnp.float32), 0.1, 1.9),
        "w_query": centred(splits[6], (C, C), (C // 16) ** -0.5, 1.5),
        "w_key": centred(splits[7], (C, C), C ** -0.5, 0.375),
        "w_value": centred(splits[8], (C, C), C ** -0.5, 0.375),
        "w_out": centred(splits[9], (C, C), C ** -0.5, 0.375),
    }


def embed(timestep):
    half = TE // 2
    freqs = jnp.exp(-math.log(10000.0) * jnp.arange(half, dtype=jnp.float32) / half)
    angles = timestep.astype(jnp.float32)[:, None] * freqs[None, :]
    return jnp.concatenate([jnp.cos(angles), jnp.sin(angles)], axis=1)

def reference(field, cotangent, kernel, timestep, time_weight, norm_gain, w_query, w_key, w_value, w_out):
    xf = field.astype(jnp.float32)
    sig = jax.nn.sigmoid(xf)
    act = (xf * sig).astype(jnp.bfloat16)
    act_pad = jnp.pad(act, ((1, 1), (1, 1), (0, 0)))
    cot_pad = jnp.pad(cotangent, ((1, 1), (1, 1), (0, 0)))
    cot_flat = cotangent.reshape(-1, C)
    conv = jnp.zeros((NH * NW, C), jnp.float32)
    back = jnp.zeros((NH * NW, C), jnp.float32)
    grads = []
    for row_off in range(3):
        for col_off in range(3):
            tap = row_off * 3 + col_off
            window = act_pad[row_off:row_off + NH, col_off:col_off + NW].reshape(-1, C)
            conv = conv + jnp.dot(window, kernel[tap], preferred_element_type=jnp.float32)
            grads.append(lax.dot_general(window, cot_flat, (((0,), (0,)), ((), ())), preferred_element_type=jnp.float32))
            behind = cot_pad[2 - row_off:2 - row_off + NH, 2 - col_off:2 - col_off + NW].reshape(-1, C)
            back = back + lax.dot_general(behind, kernel[tap], (((1,), (1,)), ((), ())), preferred_element_type=jnp.float32)
    tbias = jnp.dot(embed(timestep), time_weight, precision=lax.Precision.HIGHEST)
    block_out = (xf + conv.reshape(NH, NW, C) + tbias).astype(jnp.bfloat16)
    grad_field = (cotangent.astype(jnp.float32) + back.reshape(NH, NW, C) * sig * (1.0 + xf * (1.0 - sig))).astype(jnp.bfloat16)
    grad_kernel = jnp.stack(grads)
    pooled = block_out.astype(jnp.float32).reshape(TH, POOL, TW, POOL, C).mean(axis=(1, 3)).reshape(-1, C)
    center = pooled - lax.optimization_barrier(jnp.mean(pooled, axis=1, keepdims=True))
    spread = lax.optimization_barrier(jnp.mean(center * center, axis=1, keepdims=True))
    normed = (center * lax.rsqrt(spread + 1e-05) * norm_gain).astype(jnp.bfloat16)
    query = jnp.dot(normed, w_query, preferred_element_type=jnp.float32).astype(jnp.bfloat16)
    keys = jnp.dot(normed, w_key, preferred_element_type=jnp.float32).astype(jnp.bfloat16)
    values = jnp.dot(normed, w_value, preferred_element_type=jnp.float32).astype(jnp.bfloat16)
    heads = C // HEAD_DIM
    q3 = query.reshape(-1, heads, HEAD_DIM).astype(jnp.float32)
    k3 = keys.reshape(-1, heads, HEAD_DIM).astype(jnp.float32)
    v3 = values.reshape(-1, heads, HEAD_DIM).astype(jnp.float32)
    scores = jnp.einsum('qhd,khd->hqk', q3, k3) / math.sqrt(HEAD_DIM)
    probs = jax.nn.softmax(scores, axis=-1).astype(jnp.bfloat16)
    mixed = jnp.einsum('hqk,khd->qhd', probs.astype(jnp.float32), v3).astype(jnp.bfloat16).reshape(-1, C)
    attended = (pooled + jnp.dot(mixed, w_out, preferred_element_type=jnp.float32)).astype(jnp.bfloat16).reshape(TH, TW, C)
    return (block_out, grad_field, grad_kernel, attended)
```

```python
import functools
import math

import jax
import jax.numpy as jnp
from jax import lax
from jax.experimental import pallas as pl
from jax.experimental.pallas import tpu as pltpu
from jax.sharding import PartitionSpec as P

HEAD_DIM = 64
TE = 256
POOL = 8
MESH = pl.DeviceIdType.MESH
F32 = jnp.float32
BF16 = jnp.bfloat16

NY, NZ, NX, NC = 4, 16, 4, 2
ROWS, COLS, C = 16, 32, 256
CELLS = ROWS * COLS
PLANE = [
    (dy, dx, dc) for dy in range(NY) for dx in range(NX) for dc in range(NC) if (dy, dx, dc) != (0, 0, 0)
]
NPLANE = len(PLANE)
NRING = NZ - 1


def device(y, z, x, c):
    return (y * 8 + z % 8, (z // 8) * 8 + x * 2 + c)


def dot(a, b):
    return jnp.dot(a, b, preferred_element_type=F32)


def dot_t(a, b):
    return lax.dot_general(a, b, (((1,), (1,)), ((), ())), preferred_element_type=F32)


def silu_rounded(v):
    return (v / (1.0 + jnp.exp(-v))).astype(BF16).astype(F32)


def send(src, dst, send_sem, recv_sem, dev):
    pltpu.make_async_remote_copy(
        src_ref=src,
        dst_ref=dst,
        send_sem=send_sem,
        recv_sem=recv_sem,
        device_id=dev,
        device_id_type=MESH,
    ).start()


def await_recv(buf, send_sem, recv_sem, dev):
    pltpu.make_async_remote_copy(
        src_ref=buf,
        dst_ref=buf,
        send_sem=send_sem,
        recv_sem=recv_sem,
        device_id=dev,
        device_id_type=MESH,
    ).wait_recv()


def await_send(buf, send_sem, recv_sem, dev):
    pltpu.make_async_remote_copy(
        src_ref=buf,
        dst_ref=buf,
        send_sem=send_sem,
        recv_sem=recv_sem,
        device_id=dev,
        device_id_type=MESH,
    ).wait_send()


def embed_bias(step, time_weight):
    half = TE // 2
    index = lax.broadcasted_iota(jnp.int32, (8, half), 1).astype(F32)
    freqs = jnp.exp(-math.log(10000.0) * index / half)
    angles = step.astype(F32) * freqs
    emb = jnp.concatenate([jnp.cos(angles), jnp.sin(angles)], axis=1)
    full = jnp.dot(emb, time_weight, precision=lax.Precision.HIGHEST, preferred_element_type=F32)
    return full[0:1, :]


def body(
    step_ref, field, cot, taps, time_weight, gain, w_query, w_key, w_value, w_out,
    block_out, grad_field, grad_kernel, attended,
    col_out, cor_out, row_in, col_in, cor_in,
    pad_act, pad_cot, win_act, win_cot,
    grads, core_in, core_sum, x_in, y_out, y_in, z_out, z_in,
    q_buf, kv_buf, part_out, part_in,
    halo_s, halo_r, group_s, group_r,
):
    lat, lon = lax.axis_index("lat"), lax.axis_index("lon")
    y, x, core = lat // 8, (lon // 2) % 4, lon % 2
    z = (lon // 8) * 8 + lat % 8

    def plane(k, sign):
        dy, dx, dc = PLANE[k]
        return device((y + sign * dy + NY) % NY, z, (x + sign * dx + NX) % NX, (core + dc) % NC)

    def ring(dz):
        return device(y, (z + dz + NZ) % NZ, x, core)

    up, down = (lat + 31) % 32, (lat + 1) % 32
    left, right = (lon + 15) % 16, (lon + 1) % 16
    corners = [(up, left), (up, right), (down, left), (down, right)]
    near = [(up, lon), (down, lon), (lat, left), (lat, right)] + corners
    other = (lat, lon + 1 - 2 * core)

    barrier = pltpu.get_barrier_semaphore()
    everyone = near + [plane(k, 1) for k in range(NPLANE)] + [ring(d) for d in range(1, NZ)]
    for dev in everyone:
        pl.semaphore_signal(barrier, inc=1, device_id=dev, device_id_type=MESH)

    cell = lax.broadcasted_iota(jnp.int32, (32, CELLS), 1)
    line = lax.broadcasted_iota(jnp.int32, (32, CELLS), 0)
    edge_cell = (line % 16) * COLS + (line // 16) * (COLS - 1)
    pick = jnp.where(cell == edge_cell, 1.0, 0.0).astype(BF16)
    flat_field = field[...].reshape(CELLS, C)
    flat_cot = cot[...].reshape(CELLS, C)
    field_cols = dot(pick, flat_field).astype(BF16)
    cot_cols = dot(pick, flat_cot).astype(BF16)
    col_out[0, 0:16, :] = field_cols[0:16]
    col_out[0, 16:32, :] = cot_cols[0:16]
    col_out[1, 0:16, :] = field_cols[16:32]
    col_out[1, 16:32, :] = cot_cols[16:32]
    corner = line // 8
    corner_cell = (corner // 2) * (CELLS - COLS) + (corner % 2) * (COLS - 1)
    pick_field = jnp.where((cell == corner_cell) & (line % 8 == 0), 1.0, 0.0).astype(BF16)
    pick_cot = jnp.where((cell == corner_cell) & (line % 8 == 1), 1.0, 0.0).astype(BF16)
    cor_out[...] = (dot(pick_field, flat_field) + dot(pick_cot, flat_cot)).reshape(4, 8, C)

    pl.semaphore_wait(barrier, len(everyone))

    sends = [
        (field.at[ROWS - 1], row_in.at[0, 0], (down, lon)),
        (cot.at[ROWS - 1], row_in.at[0, 1], (down, lon)),
        (field.at[0], row_in.at[1, 0], (up, lon)),
        (cot.at[0], row_in.at[1, 1], (up, lon)),
        (col_out.at[1], col_in.at[0], (lat, right)),
        (col_out.at[0], col_in.at[1], (lat, left)),
        (cor_out.at[3], cor_in.at[0], corners[3]),
        (cor_out.at[2], cor_in.at[1], corners[2]),
        (cor_out.at[1], cor_in.at[2], corners[1]),
        (cor_out.at[0], cor_in.at[3], corners[0]),
    ]
    copies = []
    for i, (src, dst, dev) in enumerate(sends):
        copy = pltpu.make_async_remote_copy(
            src_ref=src, dst_ref=dst, send_sem=halo_s.at[i], recv_sem=halo_r.at[i],
            device_id=dev, device_id_type=MESH,
        )
        copy.start()
        copies.append(copy)

    xf = flat_field.astype(F32)
    pad_act[1 : ROWS + 1, 8 : 8 + COLS, :] = silu_rounded(xf).reshape(ROWS, COLS, C)
    pad_cot[1 : ROWS + 1, 8 : 8 + COLS, :] = flat_cot.astype(F32).reshape(ROWS, COLS, C)
    tbias = embed_bias(step_ref[0], time_weight[...])
    row = lax.broadcasted_iota(jnp.int32, (C, C), 0)
    col = lax.broadcasted_iota(jnp.int32, (C, C), 1)
    source = (((row // 16) % 2) * 8 + ((row // 32) % 4) * 2 + row // 128) * 16 + row % 16
    reorder = jnp.where(col == source, 1.0, 0.0).astype(BF16)
    cot_t = dot_t(reorder, flat_cot).astype(BF16)

    for copy in copies:
        copy.wait_recv()
    has_up = jnp.where(lat > 0, 1.0, 0.0)
    has_down = jnp.where(lat < 31, 1.0, 0.0)
    has_left = jnp.where(lon > 0, 1.0, 0.0)
    has_right = jnp.where(lon < 15, 1.0, 0.0)
    for end, (r, has) in enumerate(((0, has_up), (ROWS + 1, has_down))):
        pad_act[r, 8 : 8 + COLS, :] = silu_rounded(row_in[end, 0].astype(F32) * has)
        pad_cot[r, 8 : 8 + COLS, :] = row_in[end, 1].astype(F32) * has
    for side, (j, has) in enumerate(((7, has_left), (8 + COLS, has_right))):
        edge = col_in[side].astype(F32) * has
        act_edge = silu_rounded(edge[0:16])
        for r in range(ROWS):
            pad_act[r + 1, j : j + 1, :] = act_edge[r : r + 1]
            pad_cot[r + 1, j : j + 1, :] = edge[16 + r : 17 + r]
    for i, (r, j, has) in enumerate((
        (0, 7, has_up * has_left),
        (0, 8 + COLS, has_up * has_right),
        (ROWS + 1, 7, has_down * has_left),
        (ROWS + 1, 8 + COLS, has_down * has_right),
    )):
        edge = cor_in[i] * has
        pad_act[r, j : j + 1, :] = silu_rounded(edge[0:1])
        pad_cot[r, j : j + 1, :] = edge[1:2]

    for b in range(3):
        win_act[b] = pad_act[:, 7 + b : 7 + b + COLS, :].astype(BF16)

    def window(ref, a, b):
        return ref[b, a : a + ROWS].reshape(CELLS, C)

    conv = xf + tbias
    for tap in range(9):
        conv = conv + dot(window(win_act, tap // 3, tap % 3), taps[tap])
    rounded = conv.astype(BF16)
    block_out[...] = rounded.reshape(ROWS, COLS, C)

    token = lax.broadcasted_iota(jnp.int32, (8, CELLS), 0)
    cell8 = lax.broadcasted_iota(jnp.int32, (8, CELLS), 1)
    its_token = (cell8 // (COLS * POOL)) * 4 + (cell8 % COLS) // POOL
    pooled = dot(jnp.where(token == its_token, 1.0, 0.0).astype(BF16), rounded) * (1.0 / (POOL * POOL))
    center = pooled - jnp.mean(pooled, axis=1, keepdims=True)
    spread = jnp.mean(center * center, axis=1, keepdims=True)
    normed = (center * lax.rsqrt(spread + 1e-05) * gain[...]).astype(BF16)
    query = dot(normed, w_query[...])
    keys = dot(normed, w_key[...])
    values = dot(normed, w_value[...])
    q_buf[NPLANE] = jnp.concatenate([query[:, 0:128], query[:, 128:256]], axis=0).astype(BF16)
    kv_buf[NRING] = jnp.concatenate([keys, values], axis=0).astype(BF16)
    for d in range(1, NZ):
        send(kv_buf.at[NRING], kv_buf.at[d - 1], group_s.at[0], group_r.at[0], ring(d))
    for k in range(NPLANE):
        send(q_buf.at[NPLANE], q_buf.at[k], group_s.at[1], group_r.at[1], plane(k, 1))

    for tap in range(9):
        part = dot(cot_t, window(win_act, tap // 3, tap % 3)).astype(BF16)
        grads[:, :, tap] = part.reshape(2, 4, 32, C)
    send(grads.at[1 - core], core_in, group_s.at[2], group_r.at[2], other)

    for b in range(3):
        win_cot[b] = pad_cot[:, 7 + b : 7 + b + COLS, :].astype(BF16)
    back = jnp.zeros((CELLS, C), F32)
    for tap in range(9):
        back = back + dot_t(window(win_cot, 2 - tap // 3, 2 - tap % 3), taps[tap])
    sig = 1.0 / (1.0 + jnp.exp(-xf))
    grad_field[...] = (
        (flat_cot.astype(F32) + back * sig * (1.0 + xf * (1.0 - sig))).astype(BF16).reshape(ROWS, COLS, C)
    )

    await_recv(core_in, group_s.at[2], group_r.at[2], other)
    core_sum[...] = (grads[core].astype(F32) + core_in[...].astype(F32)).astype(BF16)
    for k in range(1, NX):
        to = (x + k) % NX
        send(core_sum.at[to], x_in.at[k - 1], group_s.at[3], group_r.at[3], device(y, z, to, core))

    await_recv(kv_buf.at[0:NRING], group_s.at[0], group_r.at[0], other)
    await_recv(q_buf.at[0:NPLANE], group_s.at[1], group_r.at[1], other)
    nq, nk = 8 * (NPLANE + 1), 8 * NZ
    q32 = q_buf[...].astype(F32)
    kv32 = kv_buf[...].astype(F32)
    all_k = kv32[:, 0:8, :].reshape(nk, C).astype(BF16)
    all_v = kv32[:, 8:16, :].reshape(nk, C).astype(BF16)
    lane_q = lax.broadcasted_iota(jnp.int32, (nq, 128), 1)
    lane_k = lax.broadcasted_iota(jnp.int32, (nk, 128), 1)
    lse = jnp.zeros((nq, 128), F32)
    for pair in range(2):
        q2 = q32[:, 8 * pair : 8 * pair + 8, :].reshape(nq, 128)
        k2 = all_k[:, 128 * pair : 128 * pair + 128]
        v2 = all_v[:, 128 * pair : 128 * pair + 128].astype(F32)
        mixed2 = jnp.zeros((nq, 128), F32)
        for h in range(2):
            qm = jnp.where(lane_q // HEAD_DIM == h, q2, 0.0).astype(BF16)
            vm = jnp.where(lane_k // HEAD_DIM == h, v2, 0.0).astype(BF16)
            scores = dot_t(qm, k2) * (1.0 / math.sqrt(HEAD_DIM))
            top = jnp.max(scores, axis=1, keepdims=True)
            probs = jnp.exp(scores - top)
            total = jnp.sum(probs, axis=1, keepdims=True)
            mixed2 = mixed2 + dot(probs.astype(BF16), vm) * (1.0 / total)
            lse = jnp.where(lane_q // 32 == 2 * pair + h, top + jnp.log(total), lse)
        part_out[:, :, 128 * pair : 128 * pair + 128] = mixed2.reshape(NPLANE + 1, 8, 128)
    part_out[:, :, 256:384] = lse.reshape(NPLANE + 1, 8, 128)
    for k in range(NPLANE):
        send(part_out.at[k], part_in.at[k], group_s.at[4], group_r.at[4], plane(k, -1))

    await_recv(x_in, group_s.at[3], group_r.at[3], other)
    acc = core_sum[x].astype(F32)
    for k in range(NX - 1):
        acc = acc + x_in[k].astype(F32)
    lane = lax.broadcasted_iota(jnp.int32, (9 * 16, 128), 1)
    for t in range(2):
        low = acc[:, 0:16, 128 * t : 128 * t + 128].reshape(9 * 16, 128)
        high = acc[:, 16:32, 128 * t : 128 * t + 128].reshape(9 * 16, 128)
        even = jnp.where(lane < 64, low, pltpu.roll(high, 64, 1))
        odd = jnp.where(lane < 64, pltpu.roll(low, 64, 1), high)
        y_out[2 * t] = even.astype(BF16)
        y_out[2 * t + 1] = odd.astype(BF16)
    for k in range(1, NY):
        to = (y + k) % NY
        send(y_out.at[to], y_in.at[k - 1], group_s.at[5], group_r.at[5], device(to, z, x, core))

    await_recv(y_in, group_s.at[5], group_r.at[5], other)
    acc = y_out[y].astype(F32)
    for k in range(NY - 1):
        acc = acc + y_in[k].astype(F32)
    acc = jnp.concatenate([acc, jnp.zeros((256 - 144, 128), F32)], axis=0)
    z_out[...] = acc.T.reshape(NZ, 8, 256)
    for d in range(1, NZ):
        send(z_out.at[(z + d) % NZ], z_in.at[d - 1], group_s.at[6], group_r.at[6], ring(d))

    await_recv(part_in, group_s.at[4], group_r.at[4], other)
    lse = jnp.concatenate([part_in[:, :, 256:384], part_out[NPLANE:, :, 256:384]], axis=0)
    top = jnp.max(lse, axis=0, keepdims=True)
    share = jnp.exp(lse - top)
    share = (share / jnp.sum(share, axis=0, keepdims=True)).reshape(nq, 128)
    halves = []
    for pair in range(2):
        part = jnp.concatenate(
            [
                part_in[:, :, 128 * pair : 128 * pair + 128],
                part_out[NPLANE:, :, 128 * pair : 128 * pair + 128],
            ],
            axis=0,
        )
        first = share[:, 64 * pair : 64 * pair + 1]
        second = share[:, 64 * pair + 32 : 64 * pair + 33]
        weight = jnp.where(lane_q < 64, first, second).reshape(NPLANE + 1, 8, 128)
        halves.append(jnp.sum(part * weight, axis=0))
    mixed = jnp.concatenate(halves, axis=1).astype(BF16)
    attended[...] = (pooled + dot(mixed, w_out[...])).astype(BF16)

    await_recv(z_in, group_s.at[6], group_r.at[6], other)
    acc = z_out[z]
    for k in range(NRING):
        acc = acc + z_in[k]
    for tap in range(9):
        grad_kernel[tap] = acc[:, 16 * tap : 16 * tap + 16]

    for copy in copies:
        copy.wait_send()
    for i, buf in enumerate((kv_buf.at[0:NRING], q_buf.at[0:NPLANE], core_in, x_in, part_in, y_in, z_in)):
        await_send(buf, group_s.at[i], group_r.at[i], other)


def shards(
    field, cotangent, kernel, timestep, time_weight, norm_gain, w_query, w_key, w_value, w_out
):
    vmem = pl.BlockSpec(memory_space=pltpu.VMEM)
    call = pl.pallas_call(
        body,
        out_shape=(
            jax.ShapeDtypeStruct((ROWS, COLS, C), BF16),
            jax.ShapeDtypeStruct((ROWS, COLS, C), BF16),
            jax.ShapeDtypeStruct((9, 8, 16), F32),
            jax.ShapeDtypeStruct((8, C), BF16),
        ),
        in_specs=[pl.BlockSpec(memory_space=pltpu.SMEM)] + [vmem] * 9,
        out_specs=(vmem,) * 4,
        scratch_shapes=[
            pltpu.VMEM((2, 32, C), BF16),
            pltpu.VMEM((4, 8, C), F32),
            pltpu.VMEM((2, 2, COLS, C), BF16),
            pltpu.VMEM((2, 32, C), BF16),
            pltpu.VMEM((4, 8, C), F32),
            pltpu.VMEM((ROWS + 2, COLS + 16, C), F32),
            pltpu.VMEM((ROWS + 2, COLS + 16, C), F32),
            pltpu.VMEM((3, ROWS + 2, COLS, C), BF16),
            pltpu.VMEM((3, ROWS + 2, COLS, C), BF16),
            pltpu.VMEM((2, 4, 9, 32, C), BF16),
            pltpu.VMEM((4, 9, 32, C), BF16),
            pltpu.VMEM((4, 9, 32, C), BF16),
            pltpu.VMEM((NX - 1, 9, 32, C), BF16),
            pltpu.VMEM((NY, 144, 128), BF16),
            pltpu.VMEM((NY - 1, 144, 128), BF16),
            pltpu.VMEM((NZ, 8, 256), F32),
            pltpu.VMEM((NRING, 8, 256), F32),
            pltpu.VMEM((NPLANE + 1, 16, 128), BF16),
            pltpu.VMEM((NZ, 16, C), BF16),
            pltpu.VMEM((NPLANE + 1, 8, 384), F32),
            pltpu.VMEM((NPLANE, 8, 384), F32),
            pltpu.SemaphoreType.DMA((10,)),
            pltpu.SemaphoreType.DMA((10,)),
            pltpu.SemaphoreType.DMA((7,)),
            pltpu.SemaphoreType.DMA((7,)),
        ],
        compiler_params=pltpu.CompilerParams(
            collective_id=0, has_side_effects=True, vmem_limit_bytes=48 * 1024 * 1024
        ),
    )
    block_out, grad_field, grad_kernel, attended = call(
        timestep, field, cotangent, kernel, time_weight, norm_gain.reshape(1, C),
        w_query, w_key, w_value, w_out,
    )
    return block_out, grad_field, grad_kernel, attended.reshape(ROWS // POOL, COLS // POOL, C)


def solution(mesh):
    across = P("lat", "lon", None)
    return jax.shard_map(
        shards,
        mesh=mesh,
        in_specs=(across, across) + (P(),) * 8,
        out_specs=(across, across, P(None, "lat", "lon"), across),
        check_vma=False,
    )
```

```python
import functools
import math

import jax
import jax.numpy as jnp
from jax import lax
from jax.experimental import pallas as pl
from jax.experimental.pallas import tpu as pltpu
from jax.sharding import PartitionSpec as P

HEAD_DIM = 64
TE = 256
POOL = 8
MESH = pl.DeviceIdType.MESH
F32 = jnp.float32
BF16 = jnp.bfloat16

NY, NZ, NX, NC = 4, 16, 4, 2
ROWS, COLS, C = 16, 32, 256
CELLS = ROWS * COLS
PLANE = [
    (dy, dx, dc) for dy in range(NY) for dx in range(NX) for dc in range(NC) if (dy, dx, dc) != (0, 0, 0)
]
PLANE.sort(key=lambda d: -(min(d[0], NY - d[0]) + min(d[1], NX - d[1]) + 0.5 * d[2]))
NPLANE = len(PLANE)
RING = sorted(range(1, NZ), key=lambda d: -min(d, NZ - d))
NRING = NZ - 1


def device(y, z, x, c):
    return (y * 8 + z % 8, (z // 8) * 8 + x * 2 + c)


def dot(a, b):
    return jnp.dot(a, b, preferred_element_type=F32)


def dot_t(a, b):
    return lax.dot_general(a, b, (((1,), (1,)), ((), ())), preferred_element_type=F32)


def silu_rounded(v):
    return (v / (1.0 + jnp.exp(-v))).astype(BF16).astype(F32)


def send(src, dst, send_sem, recv_sem, dev):
    pltpu.make_async_remote_copy(
        src_ref=src,
        dst_ref=dst,
        send_sem=send_sem,
        recv_sem=recv_sem,
        device_id=dev,
        device_id_type=MESH,
    ).start()


def await_recv(buf, send_sem, recv_sem, dev):
    pltpu.make_async_remote_copy(
        src_ref=buf,
        dst_ref=buf,
        send_sem=send_sem,
        recv_sem=recv_sem,
        device_id=dev,
        device_id_type=MESH,
    ).wait_recv()


def await_send(buf, send_sem, recv_sem, dev):
    pltpu.make_async_remote_copy(
        src_ref=buf,
        dst_ref=buf,
        send_sem=send_sem,
        recv_sem=recv_sem,
        device_id=dev,
        device_id_type=MESH,
    ).wait_send()


def embed_bias(step, time_weight):
    half = TE // 2
    index = lax.broadcasted_iota(jnp.int32, (8, half), 1).astype(F32)
    freqs = jnp.exp(-math.log(10000.0) * index / half)
    angles = step.astype(F32) * freqs
    emb = jnp.concatenate([jnp.cos(angles), jnp.sin(angles)], axis=1)
    full = jnp.dot(emb, time_weight, precision=lax.Precision.HIGHEST, preferred_element_type=F32)
    return full[0:1, :]


def body(
    step_ref, field_hbm, cot_hbm, taps_hbm, time_weight_hbm, gain_hbm, w_query_hbm, w_key_hbm, w_value_hbm,
    w_out_hbm,
    block_out, grad_field, grad_kernel, attended,
    field, cot, taps, time_weight, gain, w_query, w_key, w_value, w_out,
    col_out, cor_out, row_in, col_in, cor_in,
    pad_act, pad_cot, win_act, win_cot,
    grads, core_in, core_sum, x_in, y_out, y_in, z_out, z_in,
    q_buf, kv_buf, part_out, part_in,
    halo_s, halo_r, group_s, group_r, load_s,
):
    loads = [
        pltpu.make_async_copy(src, dst, load_s.at[i])
        for i, (src, dst) in enumerate((
            (field_hbm, field),
            (cot_hbm, cot),
            (time_weight_hbm, time_weight),
            (taps_hbm, taps),
            (gain_hbm, gain),
            (w_query_hbm, w_query),
            (w_key_hbm, w_key),
            (w_value_hbm, w_value),
            (w_out_hbm, w_out),
        ))
    ]
    lat, lon = lax.axis_index("lat"), lax.axis_index("lon")
    y, x, core = lat // 8, (lon // 2) % 4, lon % 2
    z = (lon // 8) * 8 + lat % 8

    def plane(k, sign):
        dy, dx, dc = PLANE[k]
        return device((y + sign * dy + NY) % NY, z, (x + sign * dx + NX) % NX, (core + dc) % NC)

    def ring(dz):
        return device(y, (z + dz + NZ) % NZ, x, core)

    up, down = (lat + 31) % 32, (lat + 1) % 32
    left, right = (lon + 15) % 16, (lon + 1) % 16
    corners = [(up, left), (up, right), (down, left), (down, right)]
    near = [(up, lon), (down, lon), (lat, left), (lat, right)] + corners
    other = (lat, lon + 1 - 2 * core)

    barrier = pltpu.get_barrier_semaphore()
    everyone = near + [plane(k, 1) for k in range(NPLANE)] + [ring(d) for d in range(1, NZ)]
    for dev in everyone:
        pl.semaphore_signal(barrier, inc=1, device_id=dev, device_id_type=MESH)
    for load in loads:
        load.start()

    for load in loads[0:2]:
        load.wait()

    cell = lax.broadcasted_iota(jnp.int32, (32, CELLS), 1)
    line = lax.broadcasted_iota(jnp.int32, (32, CELLS), 0)
    edge_cell = (line % 16) * COLS + (line // 16) * (COLS - 1)
    pick = jnp.where(cell == edge_cell, 1.0, 0.0).astype(BF16)
    flat_field = field[...].reshape(CELLS, C)
    flat_cot = cot[...].reshape(CELLS, C)
    field_cols = dot(pick, flat_field).astype(BF16)
    cot_cols = dot(pick, flat_cot).astype(BF16)
    col_out[0, 0:16, :] = field_cols[0:16]
    col_out[0, 16:32, :] = cot_cols[0:16]
    col_out[1, 0:16, :] = field_cols[16:32]
    col_out[1, 16:32, :] = cot_cols[16:32]
    corner = line // 8
    corner_cell = (corner // 2) * (CELLS - COLS) + (corner % 2) * (COLS - 1)
    pick_field = jnp.where((cell == corner_cell) & (line % 8 == 0), 1.0, 0.0).astype(BF16)
    pick_cot = jnp.where((cell == corner_cell) & (line % 8 == 1), 1.0, 0.0).astype(BF16)
    cor_out[...] = (dot(pick_field, flat_field) + dot(pick_cot, flat_cot)).reshape(4, 8, C)

    pl.semaphore_wait(barrier, len(everyone))

    sends = [
        (field.at[ROWS - 1], row_in.at[0, 0], (down, lon)),
        (cot.at[ROWS - 1], row_in.at[0, 1], (down, lon)),
        (field.at[0], row_in.at[1, 0], (up, lon)),
        (cot.at[0], row_in.at[1, 1], (up, lon)),
        (col_out.at[1], col_in.at[0], (lat, right)),
        (col_out.at[0], col_in.at[1], (lat, left)),
        (cor_out.at[3], cor_in.at[0], corners[3]),
        (cor_out.at[2], cor_in.at[1], corners[2]),
        (cor_out.at[1], cor_in.at[2], corners[1]),
        (cor_out.at[0], cor_in.at[3], corners[0]),
    ]
    copies = []
    for i, (src, dst, dev) in enumerate(sends):
        copy = pltpu.make_async_remote_copy(
            src_ref=src, dst_ref=dst, send_sem=halo_s.at[i], recv_sem=halo_r.at[i],
            device_id=dev, device_id_type=MESH,
        )
        copy.start()
        copies.append(copy)

    xf = flat_field.astype(F32)
    pad_act[1 : ROWS + 1, 8 : 8 + COLS, :] = silu_rounded(xf).reshape(ROWS, COLS, C)
    pad_cot[1 : ROWS + 1, 8 : 8 + COLS, :] = flat_cot.astype(F32).reshape(ROWS, COLS, C)
    for load in loads[2:]:
        load.wait()
    tbias = embed_bias(step_ref[0], time_weight[...])
    row = lax.broadcasted_iota(jnp.int32, (C, C), 0)
    col = lax.broadcasted_iota(jnp.int32, (C, C), 1)
    source = (((row // 16) % 2) * 8 + ((row // 32) % 4) * 2 + row // 128) * 16 + row % 16
    reorder = jnp.where(col == source, 1.0, 0.0).astype(BF16)
    cot_t = dot_t(reorder, flat_cot).astype(BF16)

    for copy in copies:
        copy.wait_recv()
    has_up = jnp.where(lat > 0, 1.0, 0.0)
    has_down = jnp.where(lat < 31, 1.0, 0.0)
    has_left = jnp.where(lon > 0, 1.0, 0.0)
    has_right = jnp.where(lon < 15, 1.0, 0.0)
    for end, (r, has) in enumerate(((0, has_up), (ROWS + 1, has_down))):
        pad_act[r, 8 : 8 + COLS, :] = silu_rounded(row_in[end, 0].astype(F32) * has)
        pad_cot[r, 8 : 8 + COLS, :] = row_in[end, 1].astype(F32) * has
    for side, (j, has) in enumerate(((7, has_left), (8 + COLS, has_right))):
        edge = col_in[side].astype(F32) * has
        act_edge = silu_rounded(edge[0:16])
        for r in range(ROWS):
            pad_act[r + 1, j : j + 1, :] = act_edge[r : r + 1]
            pad_cot[r + 1, j : j + 1, :] = edge[16 + r : 17 + r]
    for i, (r, j, has) in enumerate((
        (0, 7, has_up * has_left),
        (0, 8 + COLS, has_up * has_right),
        (ROWS + 1, 7, has_down * has_left),
        (ROWS + 1, 8 + COLS, has_down * has_right),
    )):
        edge = cor_in[i] * has
        pad_act[r, j : j + 1, :] = silu_rounded(edge[0:1])
        pad_cot[r, j : j + 1, :] = edge[1:2]

    for b in range(3):
        win_act[b] = pad_act[:, 7 + b : 7 + b + COLS, :].astype(BF16)

    def window(ref, a, b):
        return ref[b, a : a + ROWS].reshape(CELLS, C)

    for tap in range(9):
        part = dot(cot_t, window(win_act, tap // 3, tap % 3)).astype(BF16)
        grads[:, :, tap] = part.reshape(2, 4, 32, C)
    send(grads.at[1 - core], core_in, group_s.at[2], group_r.at[2], other)

    conv = xf + tbias
    for tap in range(9):
        conv = conv + dot(window(win_act, tap // 3, tap % 3), taps[tap])
    rounded = conv.astype(BF16)
    block_out[...] = rounded.reshape(ROWS, COLS, C)

    token = lax.broadcasted_iota(jnp.int32, (8, CELLS), 0)
    cell8 = lax.broadcasted_iota(jnp.int32, (8, CELLS), 1)
    its_token = (cell8 // (COLS * POOL)) * 4 + (cell8 % COLS) // POOL
    pooled = dot(jnp.where(token == its_token, 1.0, 0.0).astype(BF16), rounded) * (1.0 / (POOL * POOL))
    center = pooled - jnp.mean(pooled, axis=1, keepdims=True)
    spread = jnp.mean(center * center, axis=1, keepdims=True)
    normed = (center * lax.rsqrt(spread + 1e-05) * gain[...]).astype(BF16)
    query = dot(normed, w_query[...])
    keys = dot(normed, w_key[...])
    values = dot(normed, w_value[...])
    q_buf[NPLANE] = jnp.concatenate([query[:, 0:128], query[:, 128:256]], axis=0).astype(BF16)
    kv_buf[NRING] = jnp.concatenate([keys, values], axis=0).astype(BF16)
    for d in RING:
        send(kv_buf.at[NRING], kv_buf.at[d - 1], group_s.at[0], group_r.at[0], ring(d))
    for k in range(NPLANE):
        send(q_buf.at[NPLANE], q_buf.at[k], group_s.at[1], group_r.at[1], plane(k, 1))

    await_recv(core_in, group_s.at[2], group_r.at[2], other)
    core_sum[...] = (grads[core].astype(F32) + core_in[...].astype(F32)).astype(BF16)
    for k in range(1, NX):
        to = (x + k) % NX
        send(core_sum.at[to], x_in.at[k - 1], group_s.at[3], group_r.at[3], device(y, z, to, core))

    for b in range(3):
        win_cot[b] = pad_cot[:, 7 + b : 7 + b + COLS, :].astype(BF16)
    back = jnp.zeros((CELLS, C), F32)
    for tap in range(9):
        back = back + dot_t(window(win_cot, 2 - tap // 3, 2 - tap % 3), taps[tap])
    sig = 1.0 / (1.0 + jnp.exp(-xf))
    grad_field[...] = (
        (flat_cot.astype(F32) + back * sig * (1.0 + xf * (1.0 - sig))).astype(BF16).reshape(ROWS, COLS, C)
    )

    await_recv(x_in, group_s.at[3], group_r.at[3], other)
    acc = core_sum[x].astype(F32)
    for k in range(NX - 1):
        acc = acc + x_in[k].astype(F32)
    lane = lax.broadcasted_iota(jnp.int32, (9 * 16, 128), 1)
    for t in range(2):
        low = acc[:, 0:16, 128 * t : 128 * t + 128].reshape(9 * 16, 128)
        high = acc[:, 16:32, 128 * t : 128 * t + 128].reshape(9 * 16, 128)
        even = jnp.where(lane < 64, low, pltpu.roll(high, 64, 1))
        odd = jnp.where(lane < 64, pltpu.roll(low, 64, 1), high)
        y_out[2 * t] = even.astype(BF16)
        y_out[2 * t + 1] = odd.astype(BF16)
    for k in range(1, NY):
        to = (y + k) % NY
        send(y_out.at[to], y_in.at[k - 1], group_s.at[5], group_r.at[5], device(to, z, x, core))

    await_recv(kv_buf.at[0:NRING], group_s.at[0], group_r.at[0], other)
    await_recv(q_buf.at[0:NPLANE], group_s.at[1], group_r.at[1], other)
    nq, nk = 8 * (NPLANE + 1), 8 * NZ
    q32 = q_buf[...].astype(F32)
    kv32 = kv_buf[...].astype(F32)
    all_k = kv32[:, 0:8, :].reshape(nk, C).astype(BF16)
    all_v = kv32[:, 8:16, :].reshape(nk, C).astype(BF16)
    lane_q = lax.broadcasted_iota(jnp.int32, (nq, 128), 1)
    lane_k = lax.broadcasted_iota(jnp.int32, (nk, 128), 1)
    lse = jnp.zeros((nq, 128), F32)
    for pair in range(2):
        q2 = q32[:, 8 * pair : 8 * pair + 8, :].reshape(nq, 128)
        k2 = all_k[:, 128 * pair : 128 * pair + 128]
        v2 = all_v[:, 128 * pair : 128 * pair + 128].astype(F32)
        mixed2 = jnp.zeros((nq, 128), F32)
        for h in range(2):
            qm = jnp.where(lane_q // HEAD_DIM == h, q2, 0.0).astype(BF16)
            vm = jnp.where(lane_k // HEAD_DIM == h, v2, 0.0).astype(BF16)
            scores = dot_t(qm, k2) * (1.0 / math.sqrt(HEAD_DIM))
            top = jnp.max(scores, axis=1, keepdims=True)
            probs = jnp.exp(scores - top)
            total = jnp.sum(probs, axis=1, keepdims=True)
            mixed2 = mixed2 + dot(probs.astype(BF16), vm) * (1.0 / total)
            lse = jnp.where(lane_q // 32 == 2 * pair + h, top + jnp.log(total), lse)
        part_out[:, :, 128 * pair : 128 * pair + 128] = mixed2.reshape(NPLANE + 1, 8, 128)
    part_out[:, :, 256:384] = lse.reshape(NPLANE + 1, 8, 128)
    for k in range(NPLANE):
        send(part_out.at[k], part_in.at[k], group_s.at[4], group_r.at[4], plane(k, -1))

    await_recv(y_in, group_s.at[5], group_r.at[5], other)
    acc = y_out[y].astype(F32)
    for k in range(NY - 1):
        acc = acc + y_in[k].astype(F32)
    acc = jnp.concatenate([acc, jnp.zeros((256 - 144, 128), F32)], axis=0)
    z_out[...] = acc.T.reshape(NZ, 8, 256)
    for d in RING:
        send(z_out.at[(z + d) % NZ], z_in.at[d - 1], group_s.at[6], group_r.at[6], ring(d))

    await_recv(part_in, group_s.at[4], group_r.at[4], other)
    lse = jnp.concatenate([part_in[:, :, 256:384], part_out[NPLANE:, :, 256:384]], axis=0)
    top = jnp.max(lse, axis=0, keepdims=True)
    share = jnp.exp(lse - top)
    share = (share / jnp.sum(share, axis=0, keepdims=True)).reshape(nq, 128)
    halves = []
    for pair in range(2):
        part = jnp.concatenate(
            [
                part_in[:, :, 128 * pair : 128 * pair + 128],
                part_out[NPLANE:, :, 128 * pair : 128 * pair + 128],
            ],
            axis=0,
        )
        first = share[:, 64 * pair : 64 * pair + 1]
        second = share[:, 64 * pair + 32 : 64 * pair + 33]
        weight = jnp.where(lane_q < 64, first, second).reshape(NPLANE + 1, 8, 128)
        halves.append(jnp.sum(part * weight, axis=0))
    mixed = jnp.concatenate(halves, axis=1).astype(BF16)
    result = pooled + dot(mixed, w_out[...])
    attended[0] = result[0:4].astype(BF16)
    attended[1] = result[4:8].astype(BF16)

    await_recv(z_in, group_s.at[6], group_r.at[6], other)
    acc = z_out[z]
    for k in range(NRING):
        acc = acc + z_in[k]
    for tap in range(9):
        grad_kernel[tap] = acc[:, 16 * tap : 16 * tap + 16]

    for copy in copies:
        copy.wait_send()
    for i, buf in enumerate((kv_buf.at[0:NRING], q_buf.at[0:NPLANE], core_in, x_in, part_in, y_in, z_in)):
        await_send(buf, group_s.at[i], group_r.at[i], other)


OUTS = (
    jax.ShapeDtypeStruct((ROWS, COLS, C), BF16),
    jax.ShapeDtypeStruct((ROWS, COLS, C), BF16),
    jax.ShapeDtypeStruct((9, 8, 16), F32),
    jax.ShapeDtypeStruct((ROWS // POOL, COLS // POOL, C), BF16),
)


def finish_body(*refs):
    stores = [pltpu.make_async_copy(refs[i], refs[4 + i], refs[8].at[i]) for i in range(4)]
    for store in stores:
        store.start()
    for store in stores:
        store.wait()


def finish(results):
    return pl.pallas_call(
        finish_body,
        out_shape=OUTS,
        in_specs=[pl.BlockSpec(memory_space=pltpu.VMEM)] * 4,
        out_specs=(pl.BlockSpec(memory_space=pltpu.HBM),) * 4,
        scratch_shapes=[pltpu.SemaphoreType.DMA((4,))],
        compiler_params=pltpu.CompilerParams(vmem_limit_bytes=8 * 1024 * 1024),
    )(*results)


def shards(
    field, cotangent, kernel, timestep, time_weight, norm_gain, w_query, w_key, w_value, w_out
):
    hbm = pl.BlockSpec(memory_space=pltpu.HBM)
    call = pl.pallas_call(
        body,
        out_shape=OUTS,
        in_specs=[pl.BlockSpec(memory_space=pltpu.SMEM)] + [hbm] * 9,
        out_specs=(pl.BlockSpec(memory_space=pltpu.VMEM),) * 4,
        scratch_shapes=[
            pltpu.VMEM((ROWS, COLS, C), BF16),
            pltpu.VMEM((ROWS, COLS, C), BF16),
            pltpu.VMEM((9, C, C), BF16),
            pltpu.VMEM((TE, C), F32),
            pltpu.VMEM((1, C), F32),
            pltpu.VMEM((C, C), BF16),
            pltpu.VMEM((C, C), BF16),
            pltpu.VMEM((C, C), BF16),
            pltpu.VMEM((C, C), BF16),
            pltpu.VMEM((2, 32, C), BF16),
            pltpu.VMEM((4, 8, C), F32),
            pltpu.VMEM((2, 2, COLS, C), BF16),
            pltpu.VMEM((2, 32, C), BF16),
            pltpu.VMEM((4, 8, C), F32),
            pltpu.VMEM((ROWS + 2, COLS + 16, C), F32),
            pltpu.VMEM((ROWS + 2, COLS + 16, C), F32),
            pltpu.VMEM((3, ROWS + 2, COLS, C), BF16),
            pltpu.VMEM((3, ROWS + 2, COLS, C), BF16),
            pltpu.VMEM((2, 4, 9, 32, C), BF16),
            pltpu.VMEM((4, 9, 32, C), BF16),
            pltpu.VMEM((4, 9, 32, C), BF16),
            pltpu.VMEM((NX - 1, 9, 32, C), BF16),
            pltpu.VMEM((NY, 144, 128), BF16),
            pltpu.VMEM((NY - 1, 144, 128), BF16),
            pltpu.VMEM((NZ, 8, 256), F32),
            pltpu.VMEM((NRING, 8, 256), F32),
            pltpu.VMEM((NPLANE + 1, 16, 128), BF16),
            pltpu.VMEM((NZ, 16, C), BF16),
            pltpu.VMEM((NPLANE + 1, 8, 384), F32),
            pltpu.VMEM((NPLANE, 8, 384), F32),
            pltpu.SemaphoreType.DMA((10,)),
            pltpu.SemaphoreType.DMA((10,)),
            pltpu.SemaphoreType.DMA((7,)),
            pltpu.SemaphoreType.DMA((7,)),
            pltpu.SemaphoreType.DMA((9,)),
        ],
        compiler_params=pltpu.CompilerParams(
            collective_id=0, has_side_effects=True, vmem_limit_bytes=40 * 1024 * 1024
        ),
    )
    operands = (
        field, cotangent, kernel, time_weight, norm_gain.reshape(1, C), w_query, w_key, w_value, w_out
    )
    results = call(timestep, *(pltpu.with_memory_space_constraint(v, pltpu.HBM) for v in operands))
    return finish(results)


def solution(mesh):
    across = P("lat", "lon", None)
    return jax.shard_map(
        shards,
        mesh=mesh,
        in_specs=(across, across) + (P(),) * 8,
        out_specs=(across, across, P(None, "lat", "lon"), across),
        check_vma=False,
    )
```

```python
import functools
import math

import jax
import jax.numpy as jnp
from jax import lax
from jax.experimental import pallas as pl
from jax.experimental.pallas import tpu as pltpu
from jax.sharding import PartitionSpec as P

HEAD_DIM = 64
TE = 256
POOL = 8
MESH = pl.DeviceIdType.MESH
F32 = jnp.float32
BF16 = jnp.bfloat16

NY, NZ, NX, NC = 4, 16, 4, 2
ROWS, COLS, C = 16, 32, 256
CELLS = ROWS * COLS
TAPS_P = 5
PLANE = [
    (dy, dx, dc) for dy in range(NY) for dx in range(NX) for dc in range(NC) if (dy, dx, dc) != (0, 0, 0)
]
PLANE.sort(key=lambda d: -(min(d[0], NY - d[0]) + min(d[1], NX - d[1]) + 0.5 * d[2]))
NPLANE = len(PLANE)
RING = sorted(range(1, NZ), key=lambda d: -min(d, NZ - d))
NRING = NZ - 1


def device(y, z, x, c):
    return (y * 8 + z % 8, (z // 8) * 8 + x * 2 + c)


def dot(a, b):
    return jnp.dot(a, b, preferred_element_type=F32)


def dot_t(a, b):
    return lax.dot_general(a, b, (((1,), (1,)), ((), ())), preferred_element_type=F32)


def silu_rounded(v):
    return (v / (1.0 + jnp.exp(-v))).astype(BF16).astype(F32)


def send(src, dst, send_sem, recv_sem, dev):
    pltpu.make_async_remote_copy(
        src_ref=src,
        dst_ref=dst,
        send_sem=send_sem,
        recv_sem=recv_sem,
        device_id=dev,
        device_id_type=MESH,
    ).start()


def await_recv(buf, send_sem, recv_sem, dev):
    pltpu.make_async_remote_copy(
        src_ref=buf,
        dst_ref=buf,
        send_sem=send_sem,
        recv_sem=recv_sem,
        device_id=dev,
        device_id_type=MESH,
    ).wait_recv()


def await_send(buf, send_sem, recv_sem, dev):
    pltpu.make_async_remote_copy(
        src_ref=buf,
        dst_ref=buf,
        send_sem=send_sem,
        recv_sem=recv_sem,
        device_id=dev,
        device_id_type=MESH,
    ).wait_send()


def by_y(cells):
    rows = 16 * cells.shape[0]
    lane = lax.broadcasted_iota(jnp.int32, (rows, 128), 1)
    blocks = []
    for t in range(2):
        low = cells[:, 0:16, 128 * t : 128 * t + 128].reshape(rows, 128)
        high = cells[:, 16:32, 128 * t : 128 * t + 128].reshape(rows, 128)
        blocks.append(jnp.where(lane < 64, low, pltpu.roll(high, 64, 1)))
        blocks.append(jnp.where(lane < 64, pltpu.roll(low, 64, 1), high))
    return blocks


def embed_bias(step, time_weight):
    half = TE // 2
    index = lax.broadcasted_iota(jnp.int32, (8, half), 1).astype(F32)
    freqs = jnp.exp(-math.log(10000.0) * index / half)
    angles = step.astype(F32) * freqs
    emb = jnp.concatenate([jnp.cos(angles), jnp.sin(angles)], axis=1)
    full = jnp.dot(emb, time_weight, precision=lax.Precision.HIGHEST, preferred_element_type=F32)
    return full[0:1, :]


def body(
    step_ref, field_hbm, cot_hbm, taps_hbm, time_weight_hbm, gain_hbm, w_query_hbm, w_key_hbm, w_value_hbm,
    w_out_hbm,
    block_out, grad_field, grad_kernel, attended,
    field, cot, taps, time_weight, gain, w_query, w_key, w_value, w_out,
    col_out, cor_out, row_in, col_in, cor_in,
    pad_act, pad_cot, win_act, win_cot,
    grads_p, core_in_p, x_out_p, x_in_p, y_out_p, y_in_p,
    grads_q, core_in_q, y_out_q, y_in_q, x_out_q, x_in_q, z_out, z_in,
    q_buf, kv_buf, part_out, part_in,
    halo_s, halo_r, group_s, group_r, load_s,
):
    loads = [
        pltpu.make_async_copy(src, dst, load_s.at[i])
        for i, (src, dst) in enumerate((
            (field_hbm, field),
            (cot_hbm, cot),
            (time_weight_hbm, time_weight),
            (taps_hbm, taps),
            (gain_hbm, gain),
            (w_query_hbm, w_query),
            (w_key_hbm, w_key),
            (w_value_hbm, w_value),
            (w_out_hbm, w_out),
        ))
    ]
    lat, lon = lax.axis_index("lat"), lax.axis_index("lon")
    y, x, core = lat // 8, (lon // 2) % 4, lon % 2
    z = (lon // 8) * 8 + lat % 8

    def plane(k, sign):
        dy, dx, dc = PLANE[k]
        return device((y + sign * dy + NY) % NY, z, (x + sign * dx + NX) % NX, (core + dc) % NC)

    def ring(dz):
        return device(y, (z + dz + NZ) % NZ, x, core)

    up, down = (lat + 31) % 32, (lat + 1) % 32
    left, right = (lon + 15) % 16, (lon + 1) % 16
    corners = [(up, left), (up, right), (down, left), (down, right)]
    near = [(up, lon), (down, lon), (lat, left), (lat, right)] + corners
    other = (lat, lon + 1 - 2 * core)

    barrier = pltpu.get_barrier_semaphore()
    everyone = near + [plane(k, 1) for k in range(NPLANE)] + [ring(d) for d in range(1, NZ)]
    for dev in everyone:
        pl.semaphore_signal(barrier, inc=1, device_id=dev, device_id_type=MESH)
    for load in loads:
        load.start()

    for load in loads[0:2]:
        load.wait()

    cell = lax.broadcasted_iota(jnp.int32, (32, CELLS), 1)
    line = lax.broadcasted_iota(jnp.int32, (32, CELLS), 0)
    edge_cell = (line % 16) * COLS + (line // 16) * (COLS - 1)
    pick = jnp.where(cell == edge_cell, 1.0, 0.0).astype(BF16)
    flat_field = field[...].reshape(CELLS, C)
    flat_cot = cot[...].reshape(CELLS, C)
    field_cols = dot(pick, flat_field).astype(BF16)
    cot_cols = dot(pick, flat_cot).astype(BF16)
    col_out[0, 0:16, :] = field_cols[0:16]
    col_out[0, 16:32, :] = cot_cols[0:16]
    col_out[1, 0:16, :] = field_cols[16:32]
    col_out[1, 16:32, :] = cot_cols[16:32]
    corner = line // 8
    corner_cell = (corner // 2) * (CELLS - COLS) + (corner % 2) * (COLS - 1)
    pick_field = jnp.where((cell == corner_cell) & (line % 8 == 0), 1.0, 0.0).astype(BF16)
    pick_cot = jnp.where((cell == corner_cell) & (line % 8 == 1), 1.0, 0.0).astype(BF16)
    cor_out[...] = (dot(pick_field, flat_field) + dot(pick_cot, flat_cot)).reshape(4, 8, C)

    pl.semaphore_wait(barrier, len(everyone))

    sends = [
        (field.at[ROWS - 1], row_in.at[0, 0], (down, lon)),
        (cot.at[ROWS - 1], row_in.at[0, 1], (down, lon)),
        (field.at[0], row_in.at[1, 0], (up, lon)),
        (cot.at[0], row_in.at[1, 1], (up, lon)),
        (col_out.at[1], col_in.at[0], (lat, right)),
        (col_out.at[0], col_in.at[1], (lat, left)),
        (cor_out.at[3], cor_in.at[0], corners[3]),
        (cor_out.at[2], cor_in.at[1], corners[2]),
        (cor_out.at[1], cor_in.at[2], corners[1]),
        (cor_out.at[0], cor_in.at[3], corners[0]),
    ]
    copies = []
    for i, (src, dst, dev) in enumerate(sends):
        copy = pltpu.make_async_remote_copy(
            src_ref=src, dst_ref=dst, send_sem=halo_s.at[i], recv_sem=halo_r.at[i],
            device_id=dev, device_id_type=MESH,
        )
        copy.start()
        copies.append(copy)

    xf = flat_field.astype(F32)
    pad_act[1 : ROWS + 1, 8 : 8 + COLS, :] = silu_rounded(xf).reshape(ROWS, COLS, C)
    pad_cot[1 : ROWS + 1, 8 : 8 + COLS, :] = flat_cot.astype(F32).reshape(ROWS, COLS, C)
    for load in loads[2:]:
        load.wait()
    tbias = embed_bias(step_ref[0], time_weight[...])
    row = lax.broadcasted_iota(jnp.int32, (C, C), 0)
    col = lax.broadcasted_iota(jnp.int32, (C, C), 1)
    source = (((row // 16) % 2) * 8 + ((row // 32) % 4) * 2 + row // 128) * 16 + row % 16
    reorder = jnp.where(col == source, 1.0, 0.0).astype(BF16)
    cot_t = dot_t(reorder, flat_cot).astype(BF16)

    for copy in copies:
        copy.wait_recv()
    has_up = jnp.where(lat > 0, 1.0, 0.0)
    has_down = jnp.where(lat < 31, 1.0, 0.0)
    has_left = jnp.where(lon > 0, 1.0, 0.0)
    has_right = jnp.where(lon < 15, 1.0, 0.0)
    for end, (r, has) in enumerate(((0, has_up), (ROWS + 1, has_down))):
        pad_act[r, 8 : 8 + COLS, :] = silu_rounded(row_in[end, 0].astype(F32) * has)
        pad_cot[r, 8 : 8 + COLS, :] = row_in[end, 1].astype(F32) * has
    for side, (j, has) in enumerate(((7, has_left), (8 + COLS, has_right))):
        edge = col_in[side].astype(F32) * has
        act_edge = silu_rounded(edge[0:16])
        for r in range(ROWS):
            pad_act[r + 1, j : j + 1, :] = act_edge[r : r + 1]
            pad_cot[r + 1, j : j + 1, :] = edge[16 + r : 17 + r]
    for i, (r, j, has) in enumerate((
        (0, 7, has_up * has_left),
        (0, 8 + COLS, has_up * has_right),
        (ROWS + 1, 7, has_down * has_left),
        (ROWS + 1, 8 + COLS, has_down * has_right),
    )):
        edge = cor_in[i] * has
        pad_act[r, j : j + 1, :] = silu_rounded(edge[0:1])
        pad_cot[r, j : j + 1, :] = edge[1:2]

    for b in range(3):
        win_act[b] = pad_act[:, 7 + b : 7 + b + COLS, :].astype(BF16)

    def window(ref, a, b):
        return ref[b, a : a + ROWS].reshape(CELLS, C)

    for tap in range(9):
        part = dot(cot_t, window(win_act, tap // 3, tap % 3)).astype(BF16).reshape(2, 4, 32, C)
        if tap < TAPS_P:
            grads_p[:, :, tap] = part
        else:
            grads_q[:, :, tap - TAPS_P] = part
        if tap == TAPS_P - 1:
            send(grads_p.at[1 - core], core_in_p, group_s.at[2], group_r.at[2], other)
    send(grads_q.at[1 - core], core_in_q, group_s.at[7], group_r.at[7], other)

    conv = xf + tbias
    for tap in range(9):
        conv = conv + dot(window(win_act, tap // 3, tap % 3), taps[tap])
    rounded = conv.astype(BF16)
    block_out[...] = rounded.reshape(ROWS, COLS, C)

    token = lax.broadcasted_iota(jnp.int32, (8, CELLS), 0)
    cell8 = lax.broadcasted_iota(jnp.int32, (8, CELLS), 1)
    its_token = (cell8 // (COLS * POOL)) * 4 + (cell8 % COLS) // POOL
    pooled = dot(jnp.where(token == its_token, 1.0, 0.0).astype(BF16), rounded) * (1.0 / (POOL * POOL))
    center = pooled - jnp.mean(pooled, axis=1, keepdims=True)
    spread = jnp.mean(center * center, axis=1, keepdims=True)
    normed = (center * lax.rsqrt(spread + 1e-05) * gain[...]).astype(BF16)
    query = dot(normed, w_query[...])
    keys = dot(normed, w_key[...])
    values = dot(normed, w_value[...])
    q_buf[NPLANE] = jnp.concatenate([query[:, 0:128], query[:, 128:256]], axis=0).astype(BF16)
    kv_buf[NRING] = jnp.concatenate([keys, values], axis=0).astype(BF16)
    for d in RING:
        send(kv_buf.at[NRING], kv_buf.at[d - 1], group_s.at[0], group_r.at[0], ring(d))

    await_recv(core_in_p, group_s.at[2], group_r.at[2], other)
    x_out_p[...] = (grads_p[core].astype(F32) + core_in_p[...].astype(F32)).astype(BF16)
    for k in (2, 1, 3):
        to = (x + k) % NX
        send(x_out_p.at[to], x_in_p.at[k - 1], group_s.at[3], group_r.at[3], device(y, z, to, core))
    await_recv(core_in_q, group_s.at[7], group_r.at[7], other)
    acc = grads_q[core].astype(F32) + core_in_q[...].astype(F32)
    for i, block in enumerate(by_y(acc.reshape(4 * (9 - TAPS_P), 32, C))):
        y_out_q[i] = block.astype(BF16)
    for k in (2, 1, 3):
        to = (y + k) % NY
        send(y_out_q.at[to], y_in_q.at[k - 1], group_s.at[8], group_r.at[8], device(to, z, x, core))
    for k in range(NPLANE):
        send(q_buf.at[NPLANE], q_buf.at[k], group_s.at[1], group_r.at[1], plane(k, 1))

    for b in range(3):
        win_cot[b] = pad_cot[:, 7 + b : 7 + b + COLS, :].astype(BF16)
    back = jnp.zeros((CELLS, C), F32)
    for tap in range(9):
        back = back + dot_t(window(win_cot, 2 - tap // 3, 2 - tap % 3), taps[tap])
    sig = 1.0 / (1.0 + jnp.exp(-xf))
    grad_field[...] = (
        (flat_cot.astype(F32) + back * sig * (1.0 + xf * (1.0 - sig))).astype(BF16).reshape(ROWS, COLS, C)
    )

    await_recv(x_in_p, group_s.at[3], group_r.at[3], other)
    acc = x_out_p[x].astype(F32)
    for k in range(NX - 1):
        acc = acc + x_in_p[k].astype(F32)
    for i, block in enumerate(by_y(acc)):
        y_out_p[i] = block.astype(BF16)
    for k in (2, 1, 3):
        to = (y + k) % NY
        send(y_out_p.at[to], y_in_p.at[k - 1], group_s.at[5], group_r.at[5], device(to, z, x, core))
    await_recv(y_in_q, group_s.at[8], group_r.at[8], other)
    acc = y_out_q[y].astype(F32)
    for k in range(NY - 1):
        acc = acc + y_in_q[k].astype(F32)
    x_out_q[...] = acc.astype(BF16).reshape(x_out_q.shape)
    for k in (2, 1, 3):
        to = (x + k) % NX
        send(x_out_q.at[to], x_in_q.at[k - 1], group_s.at[9], group_r.at[9], device(y, z, to, core))

    await_recv(kv_buf.at[0:NRING], group_s.at[0], group_r.at[0], other)
    await_recv(q_buf.at[0:NPLANE], group_s.at[1], group_r.at[1], other)
    nq, nk = 8 * (NPLANE + 1), 8 * NZ
    q32 = q_buf[...].astype(F32)
    kv32 = kv_buf[...].astype(F32)
    all_k = kv32[:, 0:8, :].reshape(nk, C).astype(BF16)
    all_v = kv32[:, 8:16, :].reshape(nk, C).astype(BF16)
    lane_q = lax.broadcasted_iota(jnp.int32, (nq, 128), 1)
    lane_k = lax.broadcasted_iota(jnp.int32, (nk, 128), 1)
    lse = jnp.zeros((nq, 128), F32)
    for pair in range(2):
        q2 = q32[:, 8 * pair : 8 * pair + 8, :].reshape(nq, 128)
        k2 = all_k[:, 128 * pair : 128 * pair + 128]
        v2 = all_v[:, 128 * pair : 128 * pair + 128].astype(F32)
        mixed2 = jnp.zeros((nq, 128), F32)
        for h in range(2):
            qm = jnp.where(lane_q // HEAD_DIM == h, q2, 0.0).astype(BF16)
            vm = jnp.where(lane_k // HEAD_DIM == h, v2, 0.0).astype(BF16)
            scores = dot_t(qm, k2) * (1.0 / math.sqrt(HEAD_DIM))
            top = jnp.max(scores, axis=1, keepdims=True)
            probs = jnp.exp(scores - top)
            total = jnp.sum(probs, axis=1, keepdims=True)
            mixed2 = mixed2 + dot(probs.astype(BF16), vm) * (1.0 / total)
            lse = jnp.where(lane_q // 32 == 2 * pair + h, top + jnp.log(total), lse)
        part_out[:, :, 128 * pair : 128 * pair + 128] = mixed2.reshape(NPLANE + 1, 8, 128)
    part_out[:, :, 256:384] = lse.reshape(NPLANE + 1, 8, 128)
    for k in range(NPLANE):
        send(part_out.at[k], part_in.at[k], group_s.at[4], group_r.at[4], plane(k, -1))

    await_recv(y_in_p, group_s.at[5], group_r.at[5], other)
    await_recv(x_in_q, group_s.at[9], group_r.at[9], other)
    acc_p = y_out_p[y].astype(F32)
    acc_q = x_out_q[x].astype(F32)
    for k in range(NY - 1):
        acc_p = acc_p + y_in_p[k].astype(F32)
        acc_q = acc_q + x_in_q[k].astype(F32)
    acc = jnp.concatenate([acc_p, acc_q, jnp.zeros((256 - 144, 128), F32)], axis=0).T.reshape(NZ, 8, 256)
    z_out[...] = jnp.concatenate([acc[:, :, 0:128], acc[:, :, 128:256]], axis=1).astype(BF16)
    for d in RING:
        send(z_out.at[(z + d) % NZ], z_in.at[d - 1], group_s.at[6], group_r.at[6], ring(d))

    await_recv(part_in, group_s.at[4], group_r.at[4], other)
    lse = jnp.concatenate([part_in[:, :, 256:384], part_out[NPLANE:, :, 256:384]], axis=0)
    top = jnp.max(lse, axis=0, keepdims=True)
    share = jnp.exp(lse - top)
    share = (share / jnp.sum(share, axis=0, keepdims=True)).reshape(nq, 128)
    halves = []
    for pair in range(2):
        part = jnp.concatenate(
            [
                part_in[:, :, 128 * pair : 128 * pair + 128],
                part_out[NPLANE:, :, 128 * pair : 128 * pair + 128],
            ],
            axis=0,
        )
        first = share[:, 64 * pair : 64 * pair + 1]
        second = share[:, 64 * pair + 32 : 64 * pair + 33]
        weight = jnp.where(lane_q < 64, first, second).reshape(NPLANE + 1, 8, 128)
        halves.append(jnp.sum(part * weight, axis=0))
    mixed = jnp.concatenate(halves, axis=1).astype(BF16)
    result = pooled + dot(mixed, w_out[...])
    attended[0] = result[0:4].astype(BF16)
    attended[1] = result[4:8].astype(BF16)

    await_recv(z_in, group_s.at[6], group_r.at[6], other)
    acc = z_out[z].astype(F32)
    for k in range(NRING):
        acc = acc + z_in[k].astype(F32)
    for tap in range(8):
        grad_kernel[tap] = acc[0:8, 16 * tap : 16 * tap + 16]
    grad_kernel[8] = acc[8:16, 0:16]

    for copy in copies:
        copy.wait_send()
    for i, buf in enumerate((
        kv_buf.at[0:NRING], q_buf.at[0:NPLANE], core_in_p, x_in_p, part_in, y_in_p, z_in, core_in_q, y_in_q, x_in_q
    )):
        await_send(buf, group_s.at[i], group_r.at[i], other)


OUTS = (
    jax.ShapeDtypeStruct((ROWS, COLS, C), BF16),
    jax.ShapeDtypeStruct((ROWS, COLS, C), BF16),
    jax.ShapeDtypeStruct((9, 8, 16), F32),
    jax.ShapeDtypeStruct((ROWS // POOL, COLS // POOL, C), BF16),
)


def finish_body(*refs):
    stores = [pltpu.make_async_copy(refs[i], refs[4 + i], refs[8].at[i]) for i in range(4)]
    for store in stores:
        store.start()
    for store in stores:
        store.wait()


def finish(results):
    return pl.pallas_call(
        finish_body,
        out_shape=OUTS,
        in_specs=[pl.BlockSpec(memory_space=pltpu.VMEM)] * 4,
        out_specs=(pl.BlockSpec(memory_space=pltpu.HBM),) * 4,
        scratch_shapes=[pltpu.SemaphoreType.DMA((4,))],
        compiler_params=pltpu.CompilerParams(vmem_limit_bytes=8 * 1024 * 1024),
    )(*results)


def shards(
    field, cotangent, kernel, timestep, time_weight, norm_gain, w_query, w_key, w_value, w_out
):
    hbm = pl.BlockSpec(memory_space=pltpu.HBM)
    call = pl.pallas_call(
        body,
        out_shape=OUTS,
        in_specs=[pl.BlockSpec(memory_space=pltpu.SMEM)] + [hbm] * 9,
        out_specs=(pl.BlockSpec(memory_space=pltpu.VMEM),) * 4,
        scratch_shapes=[
            pltpu.VMEM((ROWS, COLS, C), BF16),
            pltpu.VMEM((ROWS, COLS, C), BF16),
            pltpu.VMEM((9, C, C), BF16),
            pltpu.VMEM((TE, C), F32),
            pltpu.VMEM((1, C), F32),
            pltpu.VMEM((C, C), BF16),
            pltpu.VMEM((C, C), BF16),
            pltpu.VMEM((C, C), BF16),
            pltpu.VMEM((C, C), BF16),
            pltpu.VMEM((2, 32, C), BF16),
            pltpu.VMEM((4, 8, C), F32),
            pltpu.VMEM((2, 2, COLS, C), BF16),
            pltpu.VMEM((2, 32, C), BF16),
            pltpu.VMEM((4, 8, C), F32),
            pltpu.VMEM((ROWS + 2, COLS + 16, C), F32),
            pltpu.VMEM((ROWS + 2, COLS + 16, C), F32),
            pltpu.VMEM((3, ROWS + 2, COLS, C), BF16),
            pltpu.VMEM((3, ROWS + 2, COLS, C), BF16),
            pltpu.VMEM((2, 4, TAPS_P, 32, C), BF16),
            pltpu.VMEM((4, TAPS_P, 32, C), BF16),
            pltpu.VMEM((4, TAPS_P, 32, C), BF16),
            pltpu.VMEM((NX - 1, TAPS_P, 32, C), BF16),
            pltpu.VMEM((NY, TAPS_P * 16, 128), BF16),
            pltpu.VMEM((NY - 1, TAPS_P * 16, 128), BF16),
            pltpu.VMEM((2, 4, 9 - TAPS_P, 32, C), BF16),
            pltpu.VMEM((4, 9 - TAPS_P, 32, C), BF16),
            pltpu.VMEM((NY, 4 * (9 - TAPS_P) * 16, 128), BF16),
            pltpu.VMEM((NY - 1, 4 * (9 - TAPS_P) * 16, 128), BF16),
            pltpu.VMEM((NX, (9 - TAPS_P) * 16, 128), BF16),
            pltpu.VMEM((NX - 1, (9 - TAPS_P) * 16, 128), BF16),
            pltpu.VMEM((NZ, 16, 128), BF16),
            pltpu.VMEM((NRING, 16, 128), BF16),
            pltpu.VMEM((NPLANE + 1, 16, 128), BF16),
            pltpu.VMEM((NZ, 16, C), BF16),
            pltpu.VMEM((NPLANE + 1, 8, 384), F32),
            pltpu.VMEM((NPLANE, 8, 384), F32),
            pltpu.SemaphoreType.DMA((10,)),
            pltpu.SemaphoreType.DMA((10,)),
            pltpu.SemaphoreType.DMA((10,)),
            pltpu.SemaphoreType.DMA((10,)),
            pltpu.SemaphoreType.DMA((9,)),
        ],
        compiler_params=pltpu.CompilerParams(
            collective_id=0, has_side_effects=True, vmem_limit_bytes=40 * 1024 * 1024
        ),
    )
    operands = (
        field, cotangent, kernel, time_weight, norm_gain.reshape(1, C), w_query, w_key, w_value, w_out
    )
    results = call(timestep, *(pltpu.with_memory_space_constraint(v, pltpu.HBM) for v in operands))
    return finish(results)


def solution(mesh):
    across = P("lat", "lon", None)
    return jax.shard_map(
        shards,
        mesh=mesh,
        in_specs=(across, across) + (P(),) * 8,
        out_specs=(across, across, P(None, "lat", "lon"), across),
        check_vma=False,
    )
```

```python
import functools
import math

import jax
import jax.numpy as jnp
from jax import lax
from jax.experimental import pallas as pl
from jax.experimental.pallas import tpu as pltpu
from jax.sharding import PartitionSpec as P

HEAD_DIM = 64
TE = 256
POOL = 8
MESH = pl.DeviceIdType.MESH
F32 = jnp.float32
BF16 = jnp.bfloat16

NY, NZ, NX, NC = 4, 16, 4, 2
ROWS, COLS, C = 16, 32, 256
CELLS = ROWS * COLS
TAPS_P = 5
PLANE = [
    (dy, dx, dc) for dy in range(NY) for dx in range(NX) for dc in range(NC) if (dy, dx, dc) != (0, 0, 0)
]
PLANE.sort(key=lambda d: (-d[2], -(min(d[0], NY - d[0]) + min(d[1], NX - d[1]))))
NPLANE = len(PLANE)
SPREAD = sorted(
    range(NPLANE), key=lambda k: -(min(PLANE[k][0], NY - PLANE[k][0]) + min(PLANE[k][1], NX - PLANE[k][1]))
)
RING = sorted(range(1, NZ), key=lambda d: -min(d, NZ - d))
LINE = [(dz, dc) for dz in RING + [0] for dc in range(NC) if (dz, dc) != (0, 0)]
NLINE = len(LINE)
NRING = NZ - 1


def device(y, z, x, c):
    return (y * 8 + z % 8, (z // 8) * 8 + x * 2 + c)


def dot(a, b):
    return jnp.dot(a, b, preferred_element_type=F32)


def dot_t(a, b):
    return lax.dot_general(a, b, (((1,), (1,)), ((), ())), preferred_element_type=F32)


def silu_rounded(v):
    return (v / (1.0 + jnp.exp(-v))).astype(BF16).astype(F32)


def send(src, dst, send_sem, recv_sem, dev):
    pltpu.make_async_remote_copy(
        src_ref=src,
        dst_ref=dst,
        send_sem=send_sem,
        recv_sem=recv_sem,
        device_id=dev,
        device_id_type=MESH,
    ).start()


def await_recv(buf, send_sem, recv_sem, dev):
    pltpu.make_async_remote_copy(
        src_ref=buf,
        dst_ref=buf,
        send_sem=send_sem,
        recv_sem=recv_sem,
        device_id=dev,
        device_id_type=MESH,
    ).wait_recv()


def await_send(buf, send_sem, recv_sem, dev):
    pltpu.make_async_remote_copy(
        src_ref=buf,
        dst_ref=buf,
        send_sem=send_sem,
        recv_sem=recv_sem,
        device_id=dev,
        device_id_type=MESH,
    ).wait_send()


def by_y(cells):
    rows = 16 * cells.shape[0]
    lane = lax.broadcasted_iota(jnp.int32, (rows, 128), 1)
    blocks = []
    for t in range(2):
        low = cells[:, 0:16, 128 * t : 128 * t + 128].reshape(rows, 128)
        high = cells[:, 16:32, 128 * t : 128 * t + 128].reshape(rows, 128)
        blocks.append(jnp.where(lane < 64, low, pltpu.roll(high, 64, 1)))
        blocks.append(jnp.where(lane < 64, pltpu.roll(low, 64, 1), high))
    return blocks


def embed_bias(step, time_weight):
    half = TE // 2
    index = lax.broadcasted_iota(jnp.int32, (8, half), 1).astype(F32)
    freqs = jnp.exp(-math.log(10000.0) * index / half)
    angles = step.astype(F32) * freqs
    emb = jnp.concatenate([jnp.cos(angles), jnp.sin(angles)], axis=1)
    full = jnp.dot(emb, time_weight, precision=lax.Precision.HIGHEST, preferred_element_type=F32)
    return full[0:1, :]


def body(
    step_ref, field_hbm, cot_hbm, taps_hbm, time_weight_hbm, gain_hbm, w_query_hbm, w_key_hbm, w_value_hbm,
    w_out_hbm,
    block_out, grad_field, grad_kernel, attended,
    field, cot, taps, time_weight, gain, w_query, w_key, w_value, w_out,
    col_out, cor_out, row_in, col_in, cor_in,
    pad_act, pad_cot, win_act, win_cot,
    grads_p, core_in_p, x_out_p, x_in_p, y_out_p, y_in_p,
    grads_q, core_in_q, y_out_q, y_in_q, x_out_q, x_in_q, z_out, z_in,
    q_buf, kv_out, kv_buf, part_out, part_in,
    halo_s, halo_r, group_s, group_r, load_s,
):
    loads = [
        pltpu.make_async_copy(src, dst, load_s.at[i])
        for i, (src, dst) in enumerate((
            (field_hbm, field),
            (cot_hbm, cot),
            (time_weight_hbm, time_weight),
            (taps_hbm, taps),
            (gain_hbm, gain),
            (w_query_hbm, w_query),
            (w_key_hbm, w_key),
            (w_value_hbm, w_value),
            (w_out_hbm, w_out),
        ))
    ]
    lat, lon = lax.axis_index("lat"), lax.axis_index("lon")
    y, x, core = lat // 8, (lon // 2) % 4, lon % 2
    z = (lon // 8) * 8 + lat % 8

    def plane(k, sign):
        dy, dx, dc = PLANE[k]
        return device((y + sign * dy + NY) % NY, z, (x + sign * dx + NX) % NX, (core + dc) % NC)

    def ring(dz, dc=0):
        return device(y, (z + dz + NZ) % NZ, x, (core + dc) % NC)

    up, down = (lat + 31) % 32, (lat + 1) % 32
    left, right = (lon + 15) % 16, (lon + 1) % 16
    corners = [(up, left), (up, right), (down, left), (down, right)]
    near = [(up, lon), (down, lon), (lat, left), (lat, right)] + corners
    other = (lat, lon + 1 - 2 * core)

    barrier = pltpu.get_barrier_semaphore()
    everyone = near + [plane(k, 1) for k in range(NPLANE)] + [ring(*d) for d in LINE]
    for dev in everyone:
        pl.semaphore_signal(barrier, inc=1, device_id=dev, device_id_type=MESH)
    for load in loads:
        load.start()

    for load in loads[0:2]:
        load.wait()

    cell = lax.broadcasted_iota(jnp.int32, (32, CELLS), 1)
    line = lax.broadcasted_iota(jnp.int32, (32, CELLS), 0)
    edge_cell = (line % 16) * COLS + (line // 16) * (COLS - 1)
    pick = jnp.where(cell == edge_cell, 1.0, 0.0).astype(BF16)
    flat_field = field[...].reshape(CELLS, C)
    flat_cot = cot[...].reshape(CELLS, C)
    field_cols = dot(pick, flat_field).astype(BF16)
    cot_cols = dot(pick, flat_cot).astype(BF16)
    col_out[0, 0:16, :] = field_cols[0:16]
    col_out[0, 16:32, :] = cot_cols[0:16]
    col_out[1, 0:16, :] = field_cols[16:32]
    col_out[1, 16:32, :] = cot_cols[16:32]
    corner = line // 8
    corner_cell = (corner // 2) * (CELLS - COLS) + (corner % 2) * (COLS - 1)
    pick_field = jnp.where((cell == corner_cell) & (line % 8 == 0), 1.0, 0.0).astype(BF16)
    pick_cot = jnp.where((cell == corner_cell) & (line % 8 == 1), 1.0, 0.0).astype(BF16)
    cor_out[...] = (dot(pick_field, flat_field) + dot(pick_cot, flat_cot)).reshape(4, 8, C)

    pl.semaphore_wait(barrier, len(everyone))

    sends = [
        (field.at[ROWS - 1], row_in.at[0, 0], (down, lon)),
        (cot.at[ROWS - 1], row_in.at[0, 1], (down, lon)),
        (field.at[0], row_in.at[1, 0], (up, lon)),
        (cot.at[0], row_in.at[1, 1], (up, lon)),
        (col_out.at[1], col_in.at[0], (lat, right)),
        (col_out.at[0], col_in.at[1], (lat, left)),
        (cor_out.at[3], cor_in.at[0], corners[3]),
        (cor_out.at[2], cor_in.at[1], corners[2]),
        (cor_out.at[1], cor_in.at[2], corners[1]),
        (cor_out.at[0], cor_in.at[3], corners[0]),
    ]
    copies = []
    for i, (src, dst, dev) in enumerate(sends):
        copy = pltpu.make_async_remote_copy(
            src_ref=src, dst_ref=dst, send_sem=halo_s.at[i], recv_sem=halo_r.at[i],
            device_id=dev, device_id_type=MESH,
        )
        copy.start()
        copies.append(copy)

    xf = flat_field.astype(F32)
    pad_act[1 : ROWS + 1, 8 : 8 + COLS, :] = silu_rounded(xf).reshape(ROWS, COLS, C)
    pad_cot[1 : ROWS + 1, 8 : 8 + COLS, :] = flat_cot.astype(F32).reshape(ROWS, COLS, C)
    for load in loads[2:]:
        load.wait()
    tbias = embed_bias(step_ref[0], time_weight[...])
    row = lax.broadcasted_iota(jnp.int32, (C, C), 0)
    col = lax.broadcasted_iota(jnp.int32, (C, C), 1)
    source = (((row // 16) % 2) * 8 + ((row // 32) % 4) * 2 + row // 128) * 16 + row % 16
    reorder = jnp.where(col == source, 1.0, 0.0).astype(BF16)
    cot_t = dot_t(reorder, flat_cot).astype(BF16)

    for copy in copies:
        copy.wait_recv()
    has_up = jnp.where(lat > 0, 1.0, 0.0)
    has_down = jnp.where(lat < 31, 1.0, 0.0)
    has_left = jnp.where(lon > 0, 1.0, 0.0)
    has_right = jnp.where(lon < 15, 1.0, 0.0)
    for end, (r, has) in enumerate(((0, has_up), (ROWS + 1, has_down))):
        pad_act[r, 8 : 8 + COLS, :] = silu_rounded(row_in[end, 0].astype(F32) * has)
        pad_cot[r, 8 : 8 + COLS, :] = row_in[end, 1].astype(F32) * has
    for side, (j, has) in enumerate(((7, has_left), (8 + COLS, has_right))):
        edge = col_in[side].astype(F32) * has
        act_edge = silu_rounded(edge[0:16])
        for r in range(ROWS):
            pad_act[r + 1, j : j + 1, :] = act_edge[r : r + 1]
            pad_cot[r + 1, j : j + 1, :] = edge[16 + r : 17 + r]
    for i, (r, j, has) in enumerate((
        (0, 7, has_up * has_left),
        (0, 8 + COLS, has_up * has_right),
        (ROWS + 1, 7, has_down * has_left),
        (ROWS + 1, 8 + COLS, has_down * has_right),
    )):
        edge = cor_in[i] * has
        pad_act[r, j : j + 1, :] = silu_rounded(edge[0:1])
        pad_cot[r, j : j + 1, :] = edge[1:2]

    for b in range(3):
        win_act[b] = pad_act[:, 7 + b : 7 + b + COLS, :].astype(BF16)

    def window(ref, a, b):
        return ref[b, a : a + ROWS].reshape(CELLS, C)

    for tap in range(9):
        part = dot(cot_t, window(win_act, tap // 3, tap % 3)).astype(BF16).reshape(2, 4, 32, C)
        if tap < TAPS_P:
            grads_p[:, :, tap] = part
        else:
            grads_q[:, :, tap - TAPS_P] = part
        if tap == TAPS_P - 1:
            send(grads_p.at[1 - core], core_in_p, group_s.at[2], group_r.at[2], other)
    send(grads_q.at[1 - core], core_in_q, group_s.at[7], group_r.at[7], other)

    await_recv(core_in_p, group_s.at[2], group_r.at[2], other)
    x_out_p[...] = (grads_p[core].astype(F32) + core_in_p[...].astype(F32)).astype(BF16)
    for k in (2, 1, 3):
        to = (x + k) % NX
        send(x_out_p.at[to], x_in_p.at[k - 1], group_s.at[3], group_r.at[3], device(y, z, to, core))
    await_recv(core_in_q, group_s.at[7], group_r.at[7], other)
    acc = grads_q[core].astype(F32) + core_in_q[...].astype(F32)
    for i, block in enumerate(by_y(acc.reshape(4 * (9 - TAPS_P), 32, C))):
        y_out_q[i] = block.astype(BF16)
    for k in (2, 1, 3):
        to = (y + k) % NY
        send(y_out_q.at[to], y_in_q.at[k - 1], group_s.at[8], group_r.at[8], device(to, z, x, core))

    conv = xf + tbias
    for tap in range(9):
        conv = conv + dot(window(win_act, tap // 3, tap % 3), taps[tap])
    rounded = conv.astype(BF16)
    block_out[...] = rounded.reshape(ROWS, COLS, C)

    token = lax.broadcasted_iota(jnp.int32, (8, CELLS), 0)
    cell8 = lax.broadcasted_iota(jnp.int32, (8, CELLS), 1)
    its_token = (cell8 // (COLS * POOL)) * 4 + (cell8 % COLS) // POOL
    pooled = dot(jnp.where(token == its_token, 1.0, 0.0).astype(BF16), rounded) * (1.0 / (POOL * POOL))
    center = pooled - jnp.mean(pooled, axis=1, keepdims=True)
    spread = jnp.mean(center * center, axis=1, keepdims=True)
    normed = (center * lax.rsqrt(spread + 1e-05) * gain[...]).astype(BF16)
    query = dot(normed, w_query[...])
    keys = dot(normed, w_key[...])
    values = dot(normed, w_value[...])
    q_buf[NPLANE] = jnp.concatenate([query[:, 0:128], query[:, 128:256]], axis=0).astype(BF16)
    for pair in range(2):
        part = slice(128 * pair, 128 * pair + 128)
        kv_out[pair] = jnp.concatenate([keys[:, part], values[:, part]], axis=0).astype(BF16)
    kv_buf[NLINE] = kv_out[core]
    for k, d in enumerate(LINE):
        send(kv_out.at[(core + d[1]) % NC], kv_buf.at[k], group_s.at[0], group_r.at[0], ring(*d))
    for k in SPREAD:
        send(q_buf.at[NPLANE], q_buf.at[k], group_s.at[1], group_r.at[1], plane(k, 1))

    for b in range(3):
        win_cot[b] = pad_cot[:, 7 + b : 7 + b + COLS, :].astype(BF16)
    back = jnp.zeros((CELLS, C), F32)
    for tap in range(9):
        back = back + dot_t(window(win_cot, 2 - tap // 3, 2 - tap % 3), taps[tap])
    sig = 1.0 / (1.0 + jnp.exp(-xf))
    grad_field[...] = (
        (flat_cot.astype(F32) + back * sig * (1.0 + xf * (1.0 - sig))).astype(BF16).reshape(ROWS, COLS, C)
    )

    await_recv(x_in_p, group_s.at[3], group_r.at[3], other)
    acc = x_out_p[x].astype(F32)
    for k in range(NX - 1):
        acc = acc + x_in_p[k].astype(F32)
    for i, block in enumerate(by_y(acc)):
        y_out_p[i] = block.astype(BF16)
    for k in (2, 1, 3):
        to = (y + k) % NY
        send(y_out_p.at[to], y_in_p.at[k - 1], group_s.at[5], group_r.at[5], device(to, z, x, core))
    await_recv(y_in_q, group_s.at[8], group_r.at[8], other)
    acc = y_out_q[y].astype(F32)
    for k in range(NY - 1):
        acc = acc + y_in_q[k].astype(F32)
    x_out_q[...] = acc.astype(BF16).reshape(x_out_q.shape)
    for k in (2, 1, 3):
        to = (x + k) % NX
        send(x_out_q.at[to], x_in_q.at[k - 1], group_s.at[9], group_r.at[9], device(y, z, to, core))

    await_recv(y_in_p, group_s.at[5], group_r.at[5], other)
    await_recv(x_in_q, group_s.at[9], group_r.at[9], other)
    acc_p = y_out_p[y].astype(F32)
    acc_q = x_out_q[x].astype(F32)
    for k in range(NY - 1):
        acc_p = acc_p + y_in_p[k].astype(F32)
        acc_q = acc_q + x_in_q[k].astype(F32)
    acc = jnp.concatenate([acc_p, acc_q, jnp.zeros((256 - 144, 128), F32)], axis=0).T.reshape(NZ, 8, 256)
    z_out[...] = jnp.concatenate([acc[:, :, 0:128], acc[:, :, 128:256]], axis=1).astype(BF16)
    for d in RING:
        send(z_out.at[(z + d) % NZ], z_in.at[d - 1], group_s.at[6], group_r.at[6], ring(d))

    await_recv(kv_buf.at[0:NLINE], group_s.at[0], group_r.at[0], other)
    await_recv(q_buf.at[0:NPLANE], group_s.at[1], group_r.at[1], other)
    nq, nk = 8 * (NPLANE + 1), 8 * (NLINE + 1)
    q32 = q_buf[...].astype(F32)
    q2 = jnp.where(core == 0, q32[:, 0:8, :], q32[:, 8:16, :]).reshape(nq, 128)
    kv32 = kv_buf[...].astype(F32)
    k2 = kv32[:, 0:8, :].reshape(nk, 128).astype(BF16)
    v2 = kv32[:, 8:16, :].reshape(nk, 128)
    lane_q = lax.broadcasted_iota(jnp.int32, (nq, 128), 1)
    lane_k = lax.broadcasted_iota(jnp.int32, (nk, 128), 1)
    mixed2 = jnp.zeros((nq, 128), F32)
    lse = []
    for h in range(2):
        qm = jnp.where(lane_q // HEAD_DIM == h, q2, 0.0).astype(BF16)
        vm = jnp.where(lane_k // HEAD_DIM == h, v2, 0.0).astype(BF16)
        scores = dot_t(qm, k2) * (1.0 / math.sqrt(HEAD_DIM))
        top = jnp.max(scores, axis=1, keepdims=True)
        probs = jnp.exp(scores - top)
        total = jnp.sum(probs, axis=1, keepdims=True)
        mixed2 = mixed2 + dot(probs.astype(BF16), vm) * (1.0 / total)
        lse.append(top + jnp.log(total))
    rest = jnp.where(lane_q < HEAD_DIM, lse[0], lse[1])
    high = rest.astype(BF16).astype(F32)
    rest = rest - high
    middle = rest.astype(BF16).astype(F32)
    place = (lane_q % HEAD_DIM) // 16
    terms = jnp.where(place == 0, high, jnp.where(place == 1, middle, rest - middle))
    part_out[...] = jnp.concatenate(
        [mixed2.reshape(NPLANE + 1, 8, 128), terms.reshape(NPLANE + 1, 8, 128)], axis=1
    ).astype(BF16)
    for k in SPREAD:
        send(part_out.at[k], part_in.at[k], group_s.at[4], group_r.at[4], plane(k, -1))

    await_recv(part_in, group_s.at[4], group_r.at[4], other)
    parts = jnp.concatenate([part_in[...], part_out[NPLANE:]], axis=0).astype(F32)
    half = (NPLANE + 1) // 2
    lane_h = lax.broadcasted_iota(jnp.int32, (8 * half, 128), 1)
    pairs = []
    for g in range(2):
        group = parts[g * half : g * half + half]
        terms = group[:, 8:16, :].reshape(8 * half, 128)
        sums = [
            terms[:, c : c + 1] + terms[:, c + 16 : c + 17] + terms[:, c + 32 : c + 33]
            for c in (0, HEAD_DIM)
        ]
        lse = jnp.where(lane_h < HEAD_DIM, sums[0], sums[1]).reshape(half, 8, 128)
        share = jnp.exp(lse - jnp.max(lse, axis=0, keepdims=True))
        share = share / jnp.sum(share, axis=0, keepdims=True)
        pairs.append(jnp.sum(group[:, 0:8, :] * share, axis=0))
    theirs, mine = pairs
    mixed = jnp.concatenate(
        [jnp.where(core == 0, mine, theirs), jnp.where(core == 0, theirs, mine)], axis=1
    ).astype(BF16)
    result = pooled + dot(mixed, w_out[...])
    attended[0] = result[0:4].astype(BF16)
    attended[1] = result[4:8].astype(BF16)

    await_recv(z_in, group_s.at[6], group_r.at[6], other)
    acc = z_out[z].astype(F32)
    for k in range(NRING):
        acc = acc + z_in[k].astype(F32)
    for tap in range(8):
        grad_kernel[tap] = acc[0:8, 16 * tap : 16 * tap + 16]
    grad_kernel[8] = acc[8:16, 0:16]

    for copy in copies:
        copy.wait_send()
    for i, buf in enumerate((
        kv_buf.at[0:NLINE], q_buf.at[0:NPLANE], core_in_p, x_in_p, part_in, y_in_p, z_in, core_in_q, y_in_q, x_in_q
    )):
        await_send(buf, group_s.at[i], group_r.at[i], other)


OUTS = (
    jax.ShapeDtypeStruct((ROWS, COLS, C), BF16),
    jax.ShapeDtypeStruct((ROWS, COLS, C), BF16),
    jax.ShapeDtypeStruct((9, 8, 16), F32),
    jax.ShapeDtypeStruct((ROWS // POOL, COLS // POOL, C), BF16),
)


def finish_body(*refs):
    stores = [pltpu.make_async_copy(refs[i], refs[4 + i], refs[8].at[i]) for i in range(4)]
    for store in stores:
        store.start()
    for store in stores:
        store.wait()


def finish(results):
    return pl.pallas_call(
        finish_body,
        out_shape=OUTS,
        in_specs=[pl.BlockSpec(memory_space=pltpu.VMEM)] * 4,
        out_specs=(pl.BlockSpec(memory_space=pltpu.HBM),) * 4,
        scratch_shapes=[pltpu.SemaphoreType.DMA((4,))],
        compiler_params=pltpu.CompilerParams(vmem_limit_bytes=8 * 1024 * 1024),
    )(*results)


def shards(
    field, cotangent, kernel, timestep, time_weight, norm_gain, w_query, w_key, w_value, w_out
):
    hbm = pl.BlockSpec(memory_space=pltpu.HBM)
    call = pl.pallas_call(
        body,
        out_shape=OUTS,
        in_specs=[pl.BlockSpec(memory_space=pltpu.SMEM)] + [hbm] * 9,
        out_specs=(pl.BlockSpec(memory_space=pltpu.VMEM),) * 4,
        scratch_shapes=[
            pltpu.VMEM((ROWS, COLS, C), BF16),
            pltpu.VMEM((ROWS, COLS, C), BF16),
            pltpu.VMEM((9, C, C), BF16),
            pltpu.VMEM((TE, C), F32),
            pltpu.VMEM((1, C), F32),
            pltpu.VMEM((C, C), BF16),
            pltpu.VMEM((C, C), BF16),
            pltpu.VMEM((C, C), BF16),
            pltpu.VMEM((C, C), BF16),
            pltpu.VMEM((2, 32, C), BF16),
            pltpu.VMEM((4, 8, C), F32),
            pltpu.VMEM((2, 2, COLS, C), BF16),
            pltpu.VMEM((2, 32, C), BF16),
            pltpu.VMEM((4, 8, C), F32),
            pltpu.VMEM((ROWS + 2, COLS + 16, C), F32),
            pltpu.VMEM((ROWS + 2, COLS + 16, C), F32),
            pltpu.VMEM((3, ROWS + 2, COLS, C), BF16),
            pltpu.VMEM((3, ROWS + 2, COLS, C), BF16),
            pltpu.VMEM((2, 4, TAPS_P, 32, C), BF16),
            pltpu.VMEM((4, TAPS_P, 32, C), BF16),
            pltpu.VMEM((4, TAPS_P, 32, C), BF16),
            pltpu.VMEM((NX - 1, TAPS_P, 32, C), BF16),
            pltpu.VMEM((NY, TAPS_P * 16, 128), BF16),
            pltpu.VMEM((NY - 1, TAPS_P * 16, 128), BF16),
            pltpu.VMEM((2, 4, 9 - TAPS_P, 32, C), BF16),
            pltpu.VMEM((4, 9 - TAPS_P, 32, C), BF16),
            pltpu.VMEM((NY, 4 * (9 - TAPS_P) * 16, 128), BF16),
            pltpu.VMEM((NY - 1, 4 * (9 - TAPS_P) * 16, 128), BF16),
            pltpu.VMEM((NX, (9 - TAPS_P) * 16, 128), BF16),
            pltpu.VMEM((NX - 1, (9 - TAPS_P) * 16, 128), BF16),
            pltpu.VMEM((NZ, 16, 128), BF16),
            pltpu.VMEM((NRING, 16, 128), BF16),
            pltpu.VMEM((NPLANE + 1, 16, 128), BF16),
            pltpu.VMEM((2, 16, 128), BF16),
            pltpu.VMEM((NLINE + 1, 16, 128), BF16),
            pltpu.VMEM((NPLANE + 1, 16, 128), BF16),
            pltpu.VMEM((NPLANE, 16, 128), BF16),
            pltpu.SemaphoreType.DMA((10,)),
            pltpu.SemaphoreType.DMA((10,)),
            pltpu.SemaphoreType.DMA((10,)),
            pltpu.SemaphoreType.DMA((10,)),
            pltpu.SemaphoreType.DMA((9,)),
        ],
        compiler_params=pltpu.CompilerParams(
            collective_id=0, has_side_effects=True, vmem_limit_bytes=40 * 1024 * 1024
        ),
    )
    operands = (
        field, cotangent, kernel, time_weight, norm_gain.reshape(1, C), w_query, w_key, w_value, w_out
    )
    results = call(timestep, *(pltpu.with_memory_space_constraint(v, pltpu.HBM) for v in operands))
    return finish(results)


def solution(mesh):
    across = P("lat", "lon", None)
    return jax.shard_map(
        shards,
        mesh=mesh,
        in_specs=(across, across) + (P(),) * 8,
        out_specs=(across, across, P(None, "lat", "lon"), across),
        check_vma=False,
    )
```

```python
import functools
import math

import jax
import jax.numpy as jnp
from jax import lax
from jax.experimental import pallas as pl
from jax.experimental.pallas import tpu as pltpu
from jax.sharding import PartitionSpec as P

HEAD_DIM = 64
TE = 256
POOL = 8
MESH = pl.DeviceIdType.MESH
F32 = jnp.float32
BF16 = jnp.bfloat16

NY, NZ, NX, NC = 4, 16, 4, 2
ROWS, COLS, C = 16, 32, 256
CELLS = ROWS * COLS
TAPS_P = 5
PLANE = [
    (dy, dx, dc) for dy in range(NY) for dx in range(NX) for dc in range(NC) if (dy, dx, dc) != (0, 0, 0)
]
PLANE.sort(key=lambda d: (-d[2], -(min(d[0], NY - d[0]) + min(d[1], NX - d[1]))))
NPLANE = len(PLANE)
SPREAD = sorted(
    range(NPLANE), key=lambda k: -(min(PLANE[k][0], NY - PLANE[k][0]) + min(PLANE[k][1], NX - PLANE[k][1]))
)
RING = sorted(range(1, NZ), key=lambda d: -min(d, NZ - d))
LINE = [(dz, dc) for dz in RING + [0] for dc in range(NC) if (dz, dc) != (0, 0)]
NLINE = len(LINE)
NRING = NZ - 1


def device(y, z, x, c):
    return (y * 8 + z % 8, (z // 8) * 8 + x * 2 + c)


def dot(a, b):
    return jnp.dot(a, b, preferred_element_type=F32)


def dot_t(a, b):
    return lax.dot_general(a, b, (((1,), (1,)), ((), ())), preferred_element_type=F32)


def silu_rounded(v):
    return (v / (1.0 + jnp.exp(-v))).astype(BF16).astype(F32)


def send(src, dst, send_sem, recv_sem, dev):
    pltpu.make_async_remote_copy(
        src_ref=src,
        dst_ref=dst,
        send_sem=send_sem,
        recv_sem=recv_sem,
        device_id=dev,
        device_id_type=MESH,
    ).start()


def await_recv(buf, send_sem, recv_sem, dev):
    pltpu.make_async_remote_copy(
        src_ref=buf,
        dst_ref=buf,
        send_sem=send_sem,
        recv_sem=recv_sem,
        device_id=dev,
        device_id_type=MESH,
    ).wait_recv()


def await_send(buf, send_sem, recv_sem, dev):
    pltpu.make_async_remote_copy(
        src_ref=buf,
        dst_ref=buf,
        send_sem=send_sem,
        recv_sem=recv_sem,
        device_id=dev,
        device_id_type=MESH,
    ).wait_send()


def by_y(cells):
    rows = 16 * cells.shape[0]
    lane = lax.broadcasted_iota(jnp.int32, (rows, 128), 1)
    blocks = []
    for t in range(2):
        low = cells[:, 0:16, 128 * t : 128 * t + 128].reshape(rows, 128)
        high = cells[:, 16:32, 128 * t : 128 * t + 128].reshape(rows, 128)
        blocks.append(jnp.where(lane < 64, low, pltpu.roll(high, 64, 1)))
        blocks.append(jnp.where(lane < 64, pltpu.roll(low, 64, 1), high))
    return blocks


def embed_bias(step, time_weight):
    half = TE // 2
    index = lax.broadcasted_iota(jnp.int32, (8, half), 1).astype(F32)
    freqs = jnp.exp(-math.log(10000.0) * index / half)
    angles = step.astype(F32) * freqs
    emb = jnp.concatenate([jnp.cos(angles), jnp.sin(angles)], axis=1)
    full = jnp.dot(emb, time_weight, precision=lax.Precision.HIGHEST, preferred_element_type=F32)
    return full[0:1, :]


def body(
    step_ref, field_hbm, cot_hbm, taps_hbm, time_weight_hbm, gain_hbm, w_query_hbm, w_key_hbm, w_value_hbm,
    w_out_hbm,
    block_out, grad_field, grad_kernel, attended,
    field, cot, taps, time_weight, gain, w_query, w_key, w_value, w_out,
    col_out, cor_out, row_in, col_in, cor_in,
    pad_act, pad_cot, win_act, win_cot,
    grads_p, core_in_p, x_out_p, x_in_p, y_out_p, y_in_p,
    grads_q, core_in_q, y_out_q, y_in_q, x_out_q, x_in_q, z_out, z_in,
    q_buf, kv_out, kv_buf, part_out, part_in,
    halo_s, halo_r, group_s, group_r, load_s,
):
    loads = [
        pltpu.make_async_copy(src, dst, load_s.at[i])
        for i, (src, dst) in enumerate((
            (field_hbm, field),
            (cot_hbm, cot),
            (time_weight_hbm, time_weight),
            (taps_hbm, taps),
            (gain_hbm, gain),
            (w_query_hbm, w_query),
            (w_key_hbm, w_key),
            (w_value_hbm, w_value),
            (w_out_hbm, w_out),
        ))
    ]
    lat, lon = lax.axis_index("lat"), lax.axis_index("lon")
    y, x, core = lat // 8, (lon // 2) % 4, lon % 2
    z = (lon // 8) * 8 + lat % 8

    def plane(k, sign):
        dy, dx, dc = PLANE[k]
        return device((y + sign * dy + NY) % NY, z, (x + sign * dx + NX) % NX, (core + dc) % NC)

    def ring(dz, dc=0):
        return device(y, (z + dz + NZ) % NZ, x, (core + dc) % NC)

    up, down = (lat + 31) % 32, (lat + 1) % 32
    left, right = (lon + 15) % 16, (lon + 1) % 16
    corners = [(up, left), (up, right), (down, left), (down, right)]
    near = [(up, lon), (down, lon), (lat, left), (lat, right)] + corners
    other = (lat, lon + 1 - 2 * core)

    barrier = pltpu.get_barrier_semaphore()
    everyone = near + [ring(*d) for d in LINE] + [plane(k, 1) for k in SPREAD]
    for dev in everyone:
        pl.semaphore_signal(barrier, inc=1, device_id=dev, device_id_type=MESH)
    for load in loads:
        load.start()

    for load in loads[0:2]:
        load.wait()

    cell = lax.broadcasted_iota(jnp.int32, (32, CELLS), 1)
    line = lax.broadcasted_iota(jnp.int32, (32, CELLS), 0)
    edge_cell = (line % 16) * COLS + (line // 16) * (COLS - 1)
    pick = jnp.where(cell == edge_cell, 1.0, 0.0).astype(BF16)
    flat_field = field[...].reshape(CELLS, C)
    flat_cot = cot[...].reshape(CELLS, C)
    field_cols = dot(pick, flat_field).astype(BF16)
    cot_cols = dot(pick, flat_cot).astype(BF16)
    col_out[0, 0:16, :] = field_cols[0:16]
    col_out[0, 16:32, :] = cot_cols[0:16]
    col_out[1, 0:16, :] = field_cols[16:32]
    col_out[1, 16:32, :] = cot_cols[16:32]
    corner = line // 8
    corner_cell = (corner // 2) * (CELLS - COLS) + (corner % 2) * (COLS - 1)
    pick_field = jnp.where((cell == corner_cell) & (line % 8 == 0), 1.0, 0.0).astype(BF16)
    pick_cot = jnp.where((cell == corner_cell) & (line % 8 == 1), 1.0, 0.0).astype(BF16)
    cor_out[...] = (dot(pick_field, flat_field) + dot(pick_cot, flat_cot)).reshape(4, 8, C)

    pl.semaphore_wait(barrier, len(everyone))

    sends = [
        (field.at[ROWS - 1], row_in.at[0, 0], (down, lon)),
        (cot.at[ROWS - 1], row_in.at[0, 1], (down, lon)),
        (field.at[0], row_in.at[1, 0], (up, lon)),
        (cot.at[0], row_in.at[1, 1], (up, lon)),
        (col_out.at[1], col_in.at[0], (lat, right)),
        (col_out.at[0], col_in.at[1], (lat, left)),
        (cor_out.at[3], cor_in.at[0], corners[3]),
        (cor_out.at[2], cor_in.at[1], corners[2]),
        (cor_out.at[1], cor_in.at[2], corners[1]),
        (cor_out.at[0], cor_in.at[3], corners[0]),
    ]
    copies = []
    for i, (src, dst, dev) in enumerate(sends):
        copy = pltpu.make_async_remote_copy(
            src_ref=src, dst_ref=dst, send_sem=halo_s.at[i], recv_sem=halo_r.at[i],
            device_id=dev, device_id_type=MESH,
        )
        copy.start()
        copies.append(copy)

    xf = flat_field.astype(F32)
    pad_act[1 : ROWS + 1, 8 : 8 + COLS, :] = silu_rounded(xf).reshape(ROWS, COLS, C)
    pad_cot[1 : ROWS + 1, 8 : 8 + COLS, :] = flat_cot.astype(F32).reshape(ROWS, COLS, C)
    for load in loads[2:]:
        load.wait()
    tbias = embed_bias(step_ref[0], time_weight[...])
    row = lax.broadcasted_iota(jnp.int32, (C, C), 0)
    col = lax.broadcasted_iota(jnp.int32, (C, C), 1)
    source = (((row // 16) % 2) * 8 + ((row // 32) % 4) * 2 + row // 128) * 16 + row % 16
    reorder = jnp.where(col == source, 1.0, 0.0).astype(BF16)
    cot_t = dot_t(reorder, flat_cot).astype(BF16)

    for copy in copies:
        copy.wait_recv()
    has_up = jnp.where(lat > 0, 1.0, 0.0)
    has_down = jnp.where(lat < 31, 1.0, 0.0)
    has_left = jnp.where(lon > 0, 1.0, 0.0)
    has_right = jnp.where(lon < 15, 1.0, 0.0)
    for end, (r, has) in enumerate(((0, has_up), (ROWS + 1, has_down))):
        pad_act[r, 8 : 8 + COLS, :] = silu_rounded(row_in[end, 0].astype(F32) * has)
        pad_cot[r, 8 : 8 + COLS, :] = row_in[end, 1].astype(F32) * has
    for side, (j, has) in enumerate(((7, has_left), (8 + COLS, has_right))):
        edge = col_in[side].astype(F32) * has
        act_edge = silu_rounded(edge[0:16])
        for r in range(ROWS):
            pad_act[r + 1, j : j + 1, :] = act_edge[r : r + 1]
            pad_cot[r + 1, j : j + 1, :] = edge[16 + r : 17 + r]
    for i, (r, j, has) in enumerate((
        (0, 7, has_up * has_left),
        (0, 8 + COLS, has_up * has_right),
        (ROWS + 1, 7, has_down * has_left),
        (ROWS + 1, 8 + COLS, has_down * has_right),
    )):
        edge = cor_in[i] * has
        pad_act[r, j : j + 1, :] = silu_rounded(edge[0:1])
        pad_cot[r, j : j + 1, :] = edge[1:2]

    for b in range(3):
        win_act[b] = pad_act[:, 7 + b : 7 + b + COLS, :].astype(BF16)

    def window(ref, a, b):
        return ref[b, a : a + ROWS].reshape(CELLS, C)

    for tap in range(9):
        part = dot(cot_t, window(win_act, tap // 3, tap % 3)).astype(BF16).reshape(2, 4, 32, C)
        if tap < TAPS_P:
            grads_p[:, :, tap] = part
        else:
            grads_q[:, :, tap - TAPS_P] = part
        if tap == TAPS_P - 1:
            send(grads_p.at[1 - core], core_in_p, group_s.at[2], group_r.at[2], other)
    send(grads_q.at[1 - core], core_in_q, group_s.at[7], group_r.at[7], other)

    await_recv(core_in_p, group_s.at[2], group_r.at[2], other)
    x_out_p[...] = (grads_p[core].astype(F32) + core_in_p[...].astype(F32)).astype(BF16)
    for k in (2, 1, 3):
        to = (x + k) % NX
        send(x_out_p.at[to], x_in_p.at[k - 1], group_s.at[3], group_r.at[3], device(y, z, to, core))
    await_recv(core_in_q, group_s.at[7], group_r.at[7], other)
    acc = grads_q[core].astype(F32) + core_in_q[...].astype(F32)
    for i, block in enumerate(by_y(acc.reshape(4 * (9 - TAPS_P), 32, C))):
        y_out_q[i] = block.astype(BF16)
    for k in (2, 1, 3):
        to = (y + k) % NY
        send(y_out_q.at[to], y_in_q.at[k - 1], group_s.at[8], group_r.at[8], device(to, z, x, core))

    conv = xf + tbias
    for tap in range(9):
        conv = conv + dot(window(win_act, tap // 3, tap % 3), taps[tap])
    rounded = conv.astype(BF16)
    block_out[...] = rounded.reshape(ROWS, COLS, C)

    token = lax.broadcasted_iota(jnp.int32, (8, CELLS), 0)
    cell8 = lax.broadcasted_iota(jnp.int32, (8, CELLS), 1)
    its_token = (cell8 // (COLS * POOL)) * 4 + (cell8 % COLS) // POOL
    pooled = dot(jnp.where(token == its_token, 1.0, 0.0).astype(BF16), rounded) * (1.0 / (POOL * POOL))
    center = pooled - jnp.mean(pooled, axis=1, keepdims=True)
    spread = jnp.mean(center * center, axis=1, keepdims=True)
    normed = (center * lax.rsqrt(spread + 1e-05) * gain[...]).astype(BF16)
    query = dot(normed, w_query[...])
    keys = dot(normed, w_key[...])
    values = dot(normed, w_value[...])
    q_buf[NPLANE] = jnp.concatenate([query[:, 0:128], query[:, 128:256]], axis=0).astype(BF16)
    for pair in range(2):
        part = slice(128 * pair, 128 * pair + 128)
        kv_out[pair] = jnp.concatenate([keys[:, part], values[:, part]], axis=0).astype(BF16)
    kv_buf[NLINE] = kv_out[core]
    for k, d in enumerate(LINE):
        send(kv_out.at[(core + d[1]) % NC], kv_buf.at[k], group_s.at[0], group_r.at[0], ring(*d))
    for k in SPREAD:
        send(q_buf.at[NPLANE], q_buf.at[k], group_s.at[1], group_r.at[1], plane(k, 1))

    await_recv(x_in_p, group_s.at[3], group_r.at[3], other)
    acc = x_out_p[x].astype(F32)
    for k in range(NX - 1):
        acc = acc + x_in_p[k].astype(F32)
    for i, block in enumerate(by_y(acc)):
        y_out_p[i] = block.astype(BF16)
    for k in (2, 1, 3):
        to = (y + k) % NY
        send(y_out_p.at[to], y_in_p.at[k - 1], group_s.at[5], group_r.at[5], device(to, z, x, core))
    await_recv(y_in_q, group_s.at[8], group_r.at[8], other)
    acc = y_out_q[y].astype(F32)
    for k in range(NY - 1):
        acc = acc + y_in_q[k].astype(F32)
    x_out_q[...] = acc.astype(BF16).reshape(x_out_q.shape)
    for k in (2, 1, 3):
        to = (x + k) % NX
        send(x_out_q.at[to], x_in_q.at[k - 1], group_s.at[9], group_r.at[9], device(y, z, to, core))

    for b in range(3):
        win_cot[b] = pad_cot[:, 7 + b : 7 + b + COLS, :].astype(BF16)
    back = jnp.zeros((CELLS, C), F32)
    for tap in range(9):
        back = back + dot_t(window(win_cot, 2 - tap // 3, 2 - tap % 3), taps[tap])
    sig = 1.0 / (1.0 + jnp.exp(-xf))
    grad_field[...] = (
        (flat_cot.astype(F32) + back * sig * (1.0 + xf * (1.0 - sig))).astype(BF16).reshape(ROWS, COLS, C)
    )

    await_recv(y_in_p, group_s.at[5], group_r.at[5], other)
    await_recv(x_in_q, group_s.at[9], group_r.at[9], other)
    acc_p = y_out_p[y].astype(F32)
    acc_q = x_out_q[x].astype(F32)
    for k in range(NY - 1):
        acc_p = acc_p + y_in_p[k].astype(F32)
        acc_q = acc_q + x_in_q[k].astype(F32)
    acc = jnp.concatenate([acc_p, acc_q, jnp.zeros((256 - 144, 128), F32)], axis=0).T.reshape(NZ, 8, 256)
    z_out[...] = jnp.concatenate([acc[:, :, 0:128], acc[:, :, 128:256]], axis=1).astype(BF16)
    for d in RING:
        send(z_out.at[(z + d) % NZ], z_in.at[d - 1], group_s.at[6], group_r.at[6], ring(d))

    await_recv(kv_buf.at[0:NLINE], group_s.at[0], group_r.at[0], other)
    await_recv(q_buf.at[0:NPLANE], group_s.at[1], group_r.at[1], other)
    nq, nk = 8 * (NPLANE + 1), 8 * (NLINE + 1)
    q32 = q_buf[...].astype(F32)
    q2 = jnp.where(core == 0, q32[:, 0:8, :], q32[:, 8:16, :]).reshape(nq, 128)
    kv32 = kv_buf[...].astype(F32)
    k2 = kv32[:, 0:8, :].reshape(nk, 128).astype(BF16)
    v2 = kv32[:, 8:16, :].reshape(nk, 128)
    lane_q = lax.broadcasted_iota(jnp.int32, (nq, 128), 1)
    lane_k = lax.broadcasted_iota(jnp.int32, (nk, 128), 1)
    mixed2 = jnp.zeros((nq, 128), F32)
    lse = []
    for h in range(2):
        qm = jnp.where(lane_q // HEAD_DIM == h, q2, 0.0).astype(BF16)
        vm = jnp.where(lane_k // HEAD_DIM == h, v2, 0.0).astype(BF16)
        scores = dot_t(qm, k2) * (1.0 / math.sqrt(HEAD_DIM))
        top = jnp.max(scores, axis=1, keepdims=True)
        probs = jnp.exp(scores - top)
        total = jnp.sum(probs, axis=1, keepdims=True)
        mixed2 = mixed2 + dot(probs.astype(BF16), vm) * (1.0 / total)
        lse.append(top + jnp.log(total))
    rest = jnp.where(lane_q < HEAD_DIM, lse[0], lse[1])
    high = rest.astype(BF16).astype(F32)
    rest = rest - high
    middle = rest.astype(BF16).astype(F32)
    place = (lane_q % HEAD_DIM) // 16
    terms = jnp.where(place == 0, high, jnp.where(place == 1, middle, rest - middle))
    part_out[...] = jnp.concatenate(
        [mixed2.reshape(NPLANE + 1, 8, 128), terms.reshape(NPLANE + 1, 8, 128)], axis=1
    ).astype(BF16)
    for k in SPREAD:
        send(part_out.at[k], part_in.at[k], group_s.at[4], group_r.at[4], plane(k, -1))

    await_recv(part_in, group_s.at[4], group_r.at[4], other)
    parts = jnp.concatenate([part_in[...], part_out[NPLANE:]], axis=0).astype(F32)
    half = (NPLANE + 1) // 2
    lane_h = lax.broadcasted_iota(jnp.int32, (8 * half, 128), 1)
    pairs = []
    for g in range(2):
        group = parts[g * half : g * half + half]
        terms = group[:, 8:16, :].reshape(8 * half, 128)
        sums = [
            terms[:, c : c + 1] + terms[:, c + 16 : c + 17] + terms[:, c + 32 : c + 33]
            for c in (0, HEAD_DIM)
        ]
        lse = jnp.where(lane_h < HEAD_DIM, sums[0], sums[1]).reshape(half, 8, 128)
        share = jnp.exp(lse - jnp.max(lse, axis=0, keepdims=True))
        share = share / jnp.sum(share, axis=0, keepdims=True)
        pairs.append(jnp.sum(group[:, 0:8, :] * share, axis=0))
    theirs, mine = pairs
    mixed = jnp.concatenate(
        [jnp.where(core == 0, mine, theirs), jnp.where(core == 0, theirs, mine)], axis=1
    ).astype(BF16)
    result = pooled + dot(mixed, w_out[...])
    attended[0] = result[0:4].astype(BF16)
    attended[1] = result[4:8].astype(BF16)

    await_recv(z_in, group_s.at[6], group_r.at[6], other)
    acc = z_out[z].astype(F32)
    for k in range(NRING):
        acc = acc + z_in[k].astype(F32)
    for tap in range(8):
        grad_kernel[tap] = acc[0:8, 16 * tap : 16 * tap + 16]
    grad_kernel[8] = acc[8:16, 0:16]

    for copy in copies:
        copy.wait_send()
    for i, buf in enumerate((
        kv_buf.at[0:NLINE], q_buf.at[0:NPLANE], core_in_p, x_in_p, part_in, y_in_p, z_in, core_in_q, y_in_q, x_in_q
    )):
        await_send(buf, group_s.at[i], group_r.at[i], other)


OUTS = (
    jax.ShapeDtypeStruct((ROWS, COLS, C), BF16),
    jax.ShapeDtypeStruct((ROWS, COLS, C), BF16),
    jax.ShapeDtypeStruct((9, 8, 16), F32),
    jax.ShapeDtypeStruct((ROWS // POOL, COLS // POOL, C), BF16),
)


def finish_body(*refs):
    stores = [pltpu.make_async_copy(refs[i], refs[4 + i], refs[8].at[i]) for i in range(4)]
    for store in stores:
        store.start()
    for store in stores:
        store.wait()


def finish(results):
    return pl.pallas_call(
        finish_body,
        out_shape=OUTS,
        in_specs=[pl.BlockSpec(memory_space=pltpu.VMEM)] * 4,
        out_specs=(pl.BlockSpec(memory_space=pltpu.HBM),) * 4,
        scratch_shapes=[pltpu.SemaphoreType.DMA((4,))],
        compiler_params=pltpu.CompilerParams(vmem_limit_bytes=8 * 1024 * 1024),
    )(*results)


def shards(
    field, cotangent, kernel, timestep, time_weight, norm_gain, w_query, w_key, w_value, w_out
):
    hbm = pl.BlockSpec(memory_space=pltpu.HBM)
    call = pl.pallas_call(
        body,
        out_shape=OUTS,
        in_specs=[pl.BlockSpec(memory_space=pltpu.SMEM)] + [hbm] * 9,
        out_specs=(pl.BlockSpec(memory_space=pltpu.VMEM),) * 4,
        scratch_shapes=[
            pltpu.VMEM((ROWS, COLS, C), BF16),
            pltpu.VMEM((ROWS, COLS, C), BF16),
            pltpu.VMEM((9, C, C), BF16),
            pltpu.VMEM((TE, C), F32),
            pltpu.VMEM((1, C), F32),
            pltpu.VMEM((C, C), BF16),
            pltpu.VMEM((C, C), BF16),
            pltpu.VMEM((C, C), BF16),
            pltpu.VMEM((C, C), BF16),
            pltpu.VMEM((2, 32, C), BF16),
            pltpu.VMEM((4, 8, C), F32),
            pltpu.VMEM((2, 2, COLS, C), BF16),
            pltpu.VMEM((2, 32, C), BF16),
            pltpu.VMEM((4, 8, C), F32),
            pltpu.VMEM((ROWS + 2, COLS + 16, C), F32),
            pltpu.VMEM((ROWS + 2, COLS + 16, C), F32),
            pltpu.VMEM((3, ROWS + 2, COLS, C), BF16),
            pltpu.VMEM((3, ROWS + 2, COLS, C), BF16),
            pltpu.VMEM((2, 4, TAPS_P, 32, C), BF16),
            pltpu.VMEM((4, TAPS_P, 32, C), BF16),
            pltpu.VMEM((4, TAPS_P, 32, C), BF16),
            pltpu.VMEM((NX - 1, TAPS_P, 32, C), BF16),
            pltpu.VMEM((NY, TAPS_P * 16, 128), BF16),
            pltpu.VMEM((NY - 1, TAPS_P * 16, 128), BF16),
            pltpu.VMEM((2, 4, 9 - TAPS_P, 32, C), BF16),
            pltpu.VMEM((4, 9 - TAPS_P, 32, C), BF16),
            pltpu.VMEM((NY, 4 * (9 - TAPS_P) * 16, 128), BF16),
            pltpu.VMEM((NY - 1, 4 * (9 - TAPS_P) * 16, 128), BF16),
            pltpu.VMEM((NX, (9 - TAPS_P) * 16, 128), BF16),
            pltpu.VMEM((NX - 1, (9 - TAPS_P) * 16, 128), BF16),
            pltpu.VMEM((NZ, 16, 128), BF16),
            pltpu.VMEM((NRING, 16, 128), BF16),
            pltpu.VMEM((NPLANE + 1, 16, 128), BF16),
            pltpu.VMEM((2, 16, 128), BF16),
            pltpu.VMEM((NLINE + 1, 16, 128), BF16),
            pltpu.VMEM((NPLANE + 1, 16, 128), BF16),
            pltpu.VMEM((NPLANE, 16, 128), BF16),
            pltpu.SemaphoreType.DMA((10,)),
            pltpu.SemaphoreType.DMA((10,)),
            pltpu.SemaphoreType.DMA((10,)),
            pltpu.SemaphoreType.DMA((10,)),
            pltpu.SemaphoreType.DMA((9,)),
        ],
        compiler_params=pltpu.CompilerParams(
            collective_id=0, has_side_effects=True, vmem_limit_bytes=40 * 1024 * 1024
        ),
    )
    operands = (
        field, cotangent, kernel, time_weight, norm_gain.reshape(1, C), w_query, w_key, w_value, w_out
    )
    results = call(timestep, *(pltpu.with_memory_space_constraint(v, pltpu.HBM) for v in operands))
    return finish(results)


def solution(mesh):
    across = P("lat", "lon", None)
    return jax.shard_map(
        shards,
        mesh=mesh,
        in_specs=(across, across) + (P(),) * 8,
        out_specs=(across, across, P(None, "lat", "lon"), across),
        check_vma=False,
    )
```

```python
import functools
import math

import jax
import jax.numpy as jnp
from jax import lax
from jax.experimental import pallas as pl
from jax.experimental.pallas import tpu as pltpu
from jax.sharding import PartitionSpec as P

HEAD_DIM = 64
TE = 256
POOL = 8
MESH = pl.DeviceIdType.MESH
F32 = jnp.float32
BF16 = jnp.bfloat16

NY, NZ, NX, NC = 4, 16, 4, 2
ROWS, COLS, C = 16, 32, 256
CELLS = ROWS * COLS
TAPS_P = 5
PLANE = [
    (dy, dx, dc) for dy in range(NY) for dx in range(NX) for dc in range(NC) if (dy, dx, dc) != (0, 0, 0)
]
PLANE.sort(key=lambda d: (-d[2], -(min(d[0], NY - d[0]) + min(d[1], NX - d[1]))))
NPLANE = len(PLANE)
SPREAD = sorted(
    range(NPLANE), key=lambda k: -(min(PLANE[k][0], NY - PLANE[k][0]) + min(PLANE[k][1], NX - PLANE[k][1]))
)
RING = sorted(range(1, NZ), key=lambda d: -min(d, NZ - d))
LINE = [(dz, dc) for dz in RING + [0] for dc in range(NC) if (dz, dc) != (0, 0)]
NLINE = len(LINE)
NRING = NZ - 1


def device(y, z, x, c):
    return (y * 8 + z % 8, (z // 8) * 8 + x * 2 + c)


def dot(a, b):
    return jnp.dot(a, b, preferred_element_type=F32)


def dot_t(a, b):
    return lax.dot_general(a, b, (((1,), (1,)), ((), ())), preferred_element_type=F32)


def silu_rounded(v):
    return (v / (1.0 + jnp.exp(-v))).astype(BF16).astype(F32)


def send(src, dst, send_sem, recv_sem, dev):
    pltpu.make_async_remote_copy(
        src_ref=src,
        dst_ref=dst,
        send_sem=send_sem,
        recv_sem=recv_sem,
        device_id=dev,
        device_id_type=MESH,
    ).start()


def await_recv(buf, send_sem, recv_sem, dev):
    pltpu.make_async_remote_copy(
        src_ref=buf,
        dst_ref=buf,
        send_sem=send_sem,
        recv_sem=recv_sem,
        device_id=dev,
        device_id_type=MESH,
    ).wait_recv()


def await_send(buf, send_sem, recv_sem, dev):
    pltpu.make_async_remote_copy(
        src_ref=buf,
        dst_ref=buf,
        send_sem=send_sem,
        recv_sem=recv_sem,
        device_id=dev,
        device_id_type=MESH,
    ).wait_send()


def by_y(cells):
    rows = 16 * cells.shape[0]
    lane = lax.broadcasted_iota(jnp.int32, (rows, 128), 1)
    blocks = []
    for t in range(2):
        low = cells[:, 0:16, 128 * t : 128 * t + 128].reshape(rows, 128)
        high = cells[:, 16:32, 128 * t : 128 * t + 128].reshape(rows, 128)
        blocks.append(jnp.where(lane < 64, low, pltpu.roll(high, 64, 1)))
        blocks.append(jnp.where(lane < 64, pltpu.roll(low, 64, 1), high))
    return blocks


def embed_bias(step, time_weight):
    half = TE // 2
    index = lax.broadcasted_iota(jnp.int32, (8, half), 1).astype(F32)
    freqs = jnp.exp(-math.log(10000.0) * index / half)
    angles = step.astype(F32) * freqs
    emb = jnp.concatenate([jnp.cos(angles), jnp.sin(angles)], axis=1)
    full = jnp.dot(emb, time_weight, precision=lax.Precision.HIGHEST, preferred_element_type=F32)
    return full[0:1, :]


def body(
    step_ref, field_hbm, cot_hbm, taps_hbm, time_weight_hbm, gain_hbm, w_query_hbm, w_key_hbm, w_value_hbm,
    w_out_hbm,
    block_out, grad_field, grad_kernel, attended,
    field, cot, taps, time_weight, gain, w_query, w_key, w_value, w_out,
    col_out, cor_out, row_in, col_in, cor_in,
    pad_act, pad_cot, win_act, win_cot,
    grads_p, core_in_p, x_out_p, x_in_p, y_out_p, y_in_p,
    grads_q, core_in_q, y_out_q, y_in_q, x_out_q, x_in_q, z_out, z_in,
    q_buf, kv_out, kv_buf, part_out, part_in,
    halo_s, halo_r, group_s, group_r, load_s,
):
    loads = [
        pltpu.make_async_copy(src, dst, load_s.at[i])
        for i, (src, dst) in enumerate((
            (field_hbm, field),
            (cot_hbm, cot),
            (time_weight_hbm, time_weight),
            (taps_hbm, taps),
            (gain_hbm, gain),
            (w_query_hbm, w_query),
            (w_key_hbm, w_key),
            (w_value_hbm, w_value),
            (w_out_hbm, w_out),
        ))
    ]
    lat, lon = lax.axis_index("lat"), lax.axis_index("lon")
    y, x, core = lat // 8, (lon // 2) % 4, lon % 2
    z = (lon // 8) * 8 + lat % 8

    def plane(k, sign):
        dy, dx, dc = PLANE[k]
        return device((y + sign * dy + NY) % NY, z, (x + sign * dx + NX) % NX, (core + dc) % NC)

    def ring(dz, dc=0):
        return device(y, (z + dz + NZ) % NZ, x, (core + dc) % NC)

    up, down = (lat + 31) % 32, (lat + 1) % 32
    left, right = (lon + 15) % 16, (lon + 1) % 16
    corners = [(up, left), (up, right), (down, left), (down, right)]
    near = [(up, lon), (down, lon), (lat, left), (lat, right)] + corners
    other = (lat, lon + 1 - 2 * core)

    barrier = pltpu.get_barrier_semaphore()
    everyone = near + [ring(*d) for d in LINE if d != (0, 1)]
    everyone += [plane(k, 1) for k in SPREAD if PLANE[k] != (0, 0, 1)]
    for dev in everyone:
        pl.semaphore_signal(barrier, inc=1, device_id=dev, device_id_type=MESH)
    for load in loads:
        load.start()

    for load in loads[0:2]:
        load.wait()

    cell = lax.broadcasted_iota(jnp.int32, (32, CELLS), 1)
    line = lax.broadcasted_iota(jnp.int32, (32, CELLS), 0)
    edge_cell = (line % 16) * COLS + (line // 16) * (COLS - 1)
    pick = jnp.where(cell == edge_cell, 1.0, 0.0).astype(BF16)
    flat_field = field[...].reshape(CELLS, C)
    flat_cot = cot[...].reshape(CELLS, C)
    field_cols = dot(pick, flat_field).astype(BF16)
    cot_cols = dot(pick, flat_cot).astype(BF16)
    col_out[0, 0:16, :] = field_cols[0:16]
    col_out[0, 16:32, :] = cot_cols[0:16]
    col_out[1, 0:16, :] = field_cols[16:32]
    col_out[1, 16:32, :] = cot_cols[16:32]
    corner = line // 8
    corner_cell = (corner // 2) * (CELLS - COLS) + (corner % 2) * (COLS - 1)
    pick_field = jnp.where((cell == corner_cell) & (line % 8 == 0), 1.0, 0.0).astype(BF16)
    pick_cot = jnp.where((cell == corner_cell) & (line % 8 == 1), 1.0, 0.0).astype(BF16)
    cor_out[...] = (dot(pick_field, flat_field) + dot(pick_cot, flat_cot)).reshape(4, 8, C)

    pl.semaphore_wait(barrier, len(everyone))

    sends = [
        (field.at[ROWS - 1], row_in.at[0, 0], (down, lon)),
        (cot.at[ROWS - 1], row_in.at[0, 1], (down, lon)),
        (field.at[0], row_in.at[1, 0], (up, lon)),
        (cot.at[0], row_in.at[1, 1], (up, lon)),
        (col_out.at[1], col_in.at[0], (lat, right)),
        (col_out.at[0], col_in.at[1], (lat, left)),
        (cor_out.at[3], cor_in.at[0], corners[3]),
        (cor_out.at[2], cor_in.at[1], corners[2]),
        (cor_out.at[1], cor_in.at[2], corners[1]),
        (cor_out.at[0], cor_in.at[3], corners[0]),
    ]
    copies = []
    for i, (src, dst, dev) in enumerate(sends):
        copy = pltpu.make_async_remote_copy(
            src_ref=src, dst_ref=dst, send_sem=halo_s.at[i], recv_sem=halo_r.at[i],
            device_id=dev, device_id_type=MESH,
        )
        copy.start()
        copies.append(copy)

    xf = flat_field.astype(F32)
    pad_act[1 : ROWS + 1, 8 : 8 + COLS, :] = silu_rounded(xf).reshape(ROWS, COLS, C)
    pad_cot[1 : ROWS + 1, 8 : 8 + COLS, :] = flat_cot.astype(F32).reshape(ROWS, COLS, C)
    for load in loads[2:]:
        load.wait()
    tbias = embed_bias(step_ref[0], time_weight[...])
    row = lax.broadcasted_iota(jnp.int32, (C, C), 0)
    col = lax.broadcasted_iota(jnp.int32, (C, C), 1)
    source = (((row // 16) % 2) * 8 + ((row // 32) % 4) * 2 + row // 128) * 16 + row % 16
    reorder = jnp.where(col == source, 1.0, 0.0).astype(BF16)
    cot_t = dot_t(reorder, flat_cot).astype(BF16)

    for copy in copies:
        copy.wait_recv()
    has_up = jnp.where(lat > 0, 1.0, 0.0)
    has_down = jnp.where(lat < 31, 1.0, 0.0)
    has_left = jnp.where(lon > 0, 1.0, 0.0)
    has_right = jnp.where(lon < 15, 1.0, 0.0)
    for end, (r, has) in enumerate(((0, has_up), (ROWS + 1, has_down))):
        pad_act[r, 8 : 8 + COLS, :] = silu_rounded(row_in[end, 0].astype(F32) * has)
        pad_cot[r, 8 : 8 + COLS, :] = row_in[end, 1].astype(F32) * has
    for side, (j, has) in enumerate(((7, has_left), (8 + COLS, has_right))):
        edge = col_in[side].astype(F32) * has
        act_edge = silu_rounded(edge[0:16])
        for r in range(ROWS):
            pad_act[r + 1, j : j + 1, :] = act_edge[r : r + 1]
            pad_cot[r + 1, j : j + 1, :] = edge[16 + r : 17 + r]
    for i, (r, j, has) in enumerate((
        (0, 7, has_up * has_left),
        (0, 8 + COLS, has_up * has_right),
        (ROWS + 1, 7, has_down * has_left),
        (ROWS + 1, 8 + COLS, has_down * has_right),
    )):
        edge = cor_in[i] * has
        pad_act[r, j : j + 1, :] = silu_rounded(edge[0:1])
        pad_cot[r, j : j + 1, :] = edge[1:2]

    for b in range(3):
        win_act[b] = pad_act[:, 7 + b : 7 + b + COLS, :].astype(BF16)

    def window(ref, a, b):
        return ref[b, a : a + ROWS].reshape(CELLS, C)

    for tap in range(9):
        part = dot(cot_t, window(win_act, tap // 3, tap % 3)).astype(BF16).reshape(2, 4, 32, C)
        if tap < TAPS_P:
            grads_p[:, :, tap] = part
        else:
            grads_q[:, :, tap - TAPS_P] = part
        if tap == TAPS_P - 1:
            send(grads_p.at[1 - core], core_in_p, group_s.at[2], group_r.at[2], other)
    send(grads_q.at[1 - core], core_in_q, group_s.at[7], group_r.at[7], other)

    await_recv(core_in_p, group_s.at[2], group_r.at[2], other)
    x_out_p[...] = (grads_p[core].astype(F32) + core_in_p[...].astype(F32)).astype(BF16)
    for k in (2, 1, 3):
        to = (x + k) % NX
        send(x_out_p.at[to], x_in_p.at[k - 1], group_s.at[3], group_r.at[3], device(y, z, to, core))
    await_recv(core_in_q, group_s.at[7], group_r.at[7], other)
    acc = grads_q[core].astype(F32) + core_in_q[...].astype(F32)
    for i, block in enumerate(by_y(acc.reshape(4 * (9 - TAPS_P), 32, C))):
        y_out_q[i] = block.astype(BF16)
    for k in (2, 1, 3):
        to = (y + k) % NY
        send(y_out_q.at[to], y_in_q.at[k - 1], group_s.at[8], group_r.at[8], device(to, z, x, core))

    conv = xf + tbias
    for tap in range(9):
        conv = conv + dot(window(win_act, tap // 3, tap % 3), taps[tap])
    rounded = conv.astype(BF16)
    block_out[...] = rounded.reshape(ROWS, COLS, C)

    token = lax.broadcasted_iota(jnp.int32, (8, CELLS), 0)
    cell8 = lax.broadcasted_iota(jnp.int32, (8, CELLS), 1)
    its_token = (cell8 // (COLS * POOL)) * 4 + (cell8 % COLS) // POOL
    pooled = dot(jnp.where(token == its_token, 1.0, 0.0).astype(BF16), rounded) * (1.0 / (POOL * POOL))
    center = pooled - jnp.mean(pooled, axis=1, keepdims=True)
    spread = jnp.mean(center * center, axis=1, keepdims=True)
    normed = (center * lax.rsqrt(spread + 1e-05) * gain[...]).astype(BF16)
    query = dot(normed, w_query[...])
    keys = dot(normed, w_key[...])
    values = dot(normed, w_value[...])
    q_buf[NPLANE] = jnp.concatenate([query[:, 0:128], query[:, 128:256]], axis=0).astype(BF16)
    for pair in range(2):
        part = slice(128 * pair, 128 * pair + 128)
        kv_out[pair] = jnp.concatenate([keys[:, part], values[:, part]], axis=0).astype(BF16)
    kv_buf[NLINE] = kv_out[core]
    for k, d in enumerate(LINE):
        send(kv_out.at[(core + d[1]) % NC], kv_buf.at[k], group_s.at[0], group_r.at[0], ring(*d))
    for k in SPREAD:
        send(q_buf.at[NPLANE], q_buf.at[k], group_s.at[1], group_r.at[1], plane(k, 1))

    await_recv(x_in_p, group_s.at[3], group_r.at[3], other)
    acc = x_out_p[x].astype(F32)
    for k in range(NX - 1):
        acc = acc + x_in_p[k].astype(F32)
    for i, block in enumerate(by_y(acc)):
        y_out_p[i] = block.astype(BF16)
    for k in (2, 1, 3):
        to = (y + k) % NY
        send(y_out_p.at[to], y_in_p.at[k - 1], group_s.at[5], group_r.at[5], device(to, z, x, core))
    await_recv(y_in_q, group_s.at[8], group_r.at[8], other)
    acc = y_out_q[y].astype(F32)
    for k in range(NY - 1):
        acc = acc + y_in_q[k].astype(F32)
    x_out_q[...] = acc.astype(BF16).reshape(x_out_q.shape)
    for k in (2, 1, 3):
        to = (x + k) % NX
        send(x_out_q.at[to], x_in_q.at[k - 1], group_s.at[9], group_r.at[9], device(y, z, to, core))

    for b in range(3):
        win_cot[b] = pad_cot[:, 7 + b : 7 + b + COLS, :].astype(BF16)
    back = jnp.zeros((CELLS, C), F32)
    for tap in range(9):
        back = back + dot_t(window(win_cot, 2 - tap // 3, 2 - tap % 3), taps[tap])
    sig = 1.0 / (1.0 + jnp.exp(-xf))
    grad_field[...] = (
        (flat_cot.astype(F32) + back * sig * (1.0 + xf * (1.0 - sig))).astype(BF16).reshape(ROWS, COLS, C)
    )

    await_recv(y_in_p, group_s.at[5], group_r.at[5], other)
    await_recv(x_in_q, group_s.at[9], group_r.at[9], other)
    acc_p = y_out_p[y].astype(F32)
    acc_q = x_out_q[x].astype(F32)
    for k in range(NY - 1):
        acc_p = acc_p + y_in_p[k].astype(F32)
        acc_q = acc_q + x_in_q[k].astype(F32)
    acc = jnp.concatenate([acc_p, acc_q, jnp.zeros((256 - 144, 128), F32)], axis=0).T.reshape(NZ, 8, 256)
    z_out[...] = jnp.concatenate([acc[:, :, 0:128], acc[:, :, 128:256]], axis=1).astype(BF16)
    for d in RING:
        send(z_out.at[(z + d) % NZ], z_in.at[d - 1], group_s.at[6], group_r.at[6], ring(d))

    await_recv(kv_buf.at[0:NLINE], group_s.at[0], group_r.at[0], other)
    await_recv(q_buf.at[0:NPLANE], group_s.at[1], group_r.at[1], other)
    nq, nk = 8 * (NPLANE + 1), 8 * (NLINE + 1)
    q32 = q_buf[...].astype(F32)
    q2 = jnp.where(core == 0, q32[:, 0:8, :], q32[:, 8:16, :]).reshape(nq, 128)
    kv32 = kv_buf[...].astype(F32)
    k2 = kv32[:, 0:8, :].reshape(nk, 128).astype(BF16)
    v2 = kv32[:, 8:16, :].reshape(nk, 128)
    lane_q = lax.broadcasted_iota(jnp.int32, (nq, 128), 1)
    lane_k = lax.broadcasted_iota(jnp.int32, (nk, 128), 1)
    mixed2 = jnp.zeros((nq, 128), F32)
    lse = []
    for h in range(2):
        qm = jnp.where(lane_q // HEAD_DIM == h, q2, 0.0).astype(BF16)
        vm = jnp.where(lane_k // HEAD_DIM == h, v2, 0.0).astype(BF16)
        scores = dot_t(qm, k2) * (1.0 / math.sqrt(HEAD_DIM))
        top = jnp.max(scores, axis=1, keepdims=True)
        probs = jnp.exp(scores - top)
        total = jnp.sum(probs, axis=1, keepdims=True)
        mixed2 = mixed2 + dot(probs.astype(BF16), vm) * (1.0 / total)
        lse.append(top + jnp.log(total))
    rest = jnp.where(lane_q < HEAD_DIM, lse[0], lse[1])
    high = rest.astype(BF16).astype(F32)
    rest = rest - high
    middle = rest.astype(BF16).astype(F32)
    place = (lane_q % HEAD_DIM) // 16
    terms = jnp.where(place == 0, high, jnp.where(place == 1, middle, rest - middle))
    part_out[...] = jnp.concatenate(
        [mixed2.reshape(NPLANE + 1, 8, 128), terms.reshape(NPLANE + 1, 8, 128)], axis=1
    ).astype(BF16)
    for k in SPREAD:
        send(part_out.at[k], part_in.at[k], group_s.at[4], group_r.at[4], plane(k, -1))

    await_recv(part_in, group_s.at[4], group_r.at[4], other)
    parts = jnp.concatenate([part_in[...], part_out[NPLANE:]], axis=0).astype(F32)
    half = (NPLANE + 1) // 2
    lane_h = lax.broadcasted_iota(jnp.int32, (8 * half, 128), 1)
    pairs = []
    for g in range(2):
        group = parts[g * half : g * half + half]
        terms = group[:, 8:16, :].reshape(8 * half, 128)
        sums = [
            terms[:, c : c + 1] + terms[:, c + 16 : c + 17] + terms[:, c + 32 : c + 33]
            for c in (0, HEAD_DIM)
        ]
        lse = jnp.where(lane_h < HEAD_DIM, sums[0], sums[1]).reshape(half, 8, 128)
        share = jnp.exp(lse - jnp.max(lse, axis=0, keepdims=True))
        share = share / jnp.sum(share, axis=0, keepdims=True)
        pairs.append(jnp.sum(group[:, 0:8, :] * share, axis=0))
    theirs, mine = pairs
    mixed = jnp.concatenate(
        [jnp.where(core == 0, mine, theirs), jnp.where(core == 0, theirs, mine)], axis=1
    ).astype(BF16)
    result = pooled + dot(mixed, w_out[...])
    attended[0] = result[0:4].astype(BF16)
    attended[1] = result[4:8].astype(BF16)

    await_recv(z_in, group_s.at[6], group_r.at[6], other)
    acc = z_out[z].astype(F32)
    for k in range(NRING):
        acc = acc + z_in[k].astype(F32)
    for tap in range(8):
        grad_kernel[tap] = acc[0:8, 16 * tap : 16 * tap + 16]
    grad_kernel[8] = acc[8:16, 0:16]

    for copy in copies:
        copy.wait_send()
    for i, buf in enumerate((
        kv_buf.at[0:NLINE], q_buf.at[0:NPLANE], core_in_p, x_in_p, part_in, y_in_p, z_in, core_in_q, y_in_q, x_in_q
    )):
        await_send(buf, group_s.at[i], group_r.at[i], other)


OUTS = (
    jax.ShapeDtypeStruct((ROWS, COLS, C), BF16),
    jax.ShapeDtypeStruct((ROWS, COLS, C), BF16),
    jax.ShapeDtypeStruct((9, 8, 16), F32),
    jax.ShapeDtypeStruct((ROWS // POOL, COLS // POOL, C), BF16),
)


def finish_body(*refs):
    stores = [pltpu.make_async_copy(refs[i], refs[4 + i], refs[8].at[i]) for i in range(4)]
    for store in stores:
        store.start()
    for store in stores:
        store.wait()


def finish(results):
    return pl.pallas_call(
        finish_body,
        out_shape=OUTS,
        in_specs=[pl.BlockSpec(memory_space=pltpu.VMEM)] * 4,
        out_specs=(pl.BlockSpec(memory_space=pltpu.HBM),) * 4,
        scratch_shapes=[pltpu.SemaphoreType.DMA((4,))],
        compiler_params=pltpu.CompilerParams(vmem_limit_bytes=8 * 1024 * 1024),
    )(*results)


def shards(
    field, cotangent, kernel, timestep, time_weight, norm_gain, w_query, w_key, w_value, w_out
):
    hbm = pl.BlockSpec(memory_space=pltpu.HBM)
    call = pl.pallas_call(
        body,
        out_shape=OUTS,
        in_specs=[pl.BlockSpec(memory_space=pltpu.SMEM)] + [hbm] * 9,
        out_specs=(pl.BlockSpec(memory_space=pltpu.VMEM),) * 4,
        scratch_shapes=[
            pltpu.VMEM((ROWS, COLS, C), BF16),
            pltpu.VMEM((ROWS, COLS, C), BF16),
            pltpu.VMEM((9, C, C), BF16),
            pltpu.VMEM((TE, C), F32),
            pltpu.VMEM((1, C), F32),
            pltpu.VMEM((C, C), BF16),
            pltpu.VMEM((C, C), BF16),
            pltpu.VMEM((C, C), BF16),
            pltpu.VMEM((C, C), BF16),
            pltpu.VMEM((2, 32, C), BF16),
            pltpu.VMEM((4, 8, C), F32),
            pltpu.VMEM((2, 2, COLS, C), BF16),
            pltpu.VMEM((2, 32, C), BF16),
            pltpu.VMEM((4, 8, C), F32),
            pltpu.VMEM((ROWS + 2, COLS + 16, C), F32),
            pltpu.VMEM((ROWS + 2, COLS + 16, C), F32),
            pltpu.VMEM((3, ROWS + 2, COLS, C), BF16),
            pltpu.VMEM((3, ROWS + 2, COLS, C), BF16),
            pltpu.VMEM((2, 4, TAPS_P, 32, C), BF16),
            pltpu.VMEM((4, TAPS_P, 32, C), BF16),
            pltpu.VMEM((4, TAPS_P, 32, C), BF16),
            pltpu.VMEM((NX - 1, TAPS_P, 32, C), BF16),
            pltpu.VMEM((NY, TAPS_P * 16, 128), BF16),
            pltpu.VMEM((NY - 1, TAPS_P * 16, 128), BF16),
            pltpu.VMEM((2, 4, 9 - TAPS_P, 32, C), BF16),
            pltpu.VMEM((4, 9 - TAPS_P, 32, C), BF16),
            pltpu.VMEM((NY, 4 * (9 - TAPS_P) * 16, 128), BF16),
            pltpu.VMEM((NY - 1, 4 * (9 - TAPS_P) * 16, 128), BF16),
            pltpu.VMEM((NX, (9 - TAPS_P) * 16, 128), BF16),
            pltpu.VMEM((NX - 1, (9 - TAPS_P) * 16, 128), BF16),
            pltpu.VMEM((NZ, 16, 128), BF16),
            pltpu.VMEM((NRING, 16, 128), BF16),
            pltpu.VMEM((NPLANE + 1, 16, 128), BF16),
            pltpu.VMEM((2, 16, 128), BF16),
            pltpu.VMEM((NLINE + 1, 16, 128), BF16),
            pltpu.VMEM((NPLANE + 1, 16, 128), BF16),
            pltpu.VMEM((NPLANE, 16, 128), BF16),
            pltpu.SemaphoreType.DMA((10,)),
            pltpu.SemaphoreType.DMA((10,)),
            pltpu.SemaphoreType.DMA((10,)),
            pltpu.SemaphoreType.DMA((10,)),
            pltpu.SemaphoreType.DMA((9,)),
        ],
        compiler_params=pltpu.CompilerParams(
            collective_id=0, has_side_effects=True, vmem_limit_bytes=40 * 1024 * 1024
        ),
    )
    operands = (
        field, cotangent, kernel, time_weight, norm_gain.reshape(1, C), w_query, w_key, w_value, w_out
    )
    results = call(timestep, *(pltpu.with_memory_space_constraint(v, pltpu.HBM) for v in operands))
    return finish(results)


def solution(mesh):
    across = P("lat", "lon", None)
    return jax.shard_map(
        shards,
        mesh=mesh,
        in_specs=(across, across) + (P(),) * 8,
        out_specs=(across, across, P(None, "lat", "lon"), across),
        check_vma=False,
    )
```
